128 devices in a mesh: lon: 32 (over z_hi, x, y), lat: 4 (over z_lo, core).
Axes of the slice: x: 4, y: 4, z: 4 (z_hi: 2, z_lo: 2; z = z_hi * 2 + z_lo), core: 2. Of those that a mesh axis runs over, the one named last changes fastest.
Arguments:
- latents: bfloat16 [2, 144, 768, 512], P(None, 'lat', 'lon'), may hold values from -6 to 6
- region_ids: int32 [2, 144, 768], replicated, may hold values from 0 to 3
- attend_one: bfloat16 [3, 512, 512], replicated, may hold values from -1.2 to 1.2
- project_one: bfloat16 [512, 512], replicated, may hold values from -0.25 to 0.25
- expand_one: bfloat16 [512, 2048], replicated, may hold values from -0.25 to 0.25
- reduce_one: bfloat16 [2048, 512], replicated, may hold values from -0.125 to 0.125
- merge_weight: bfloat16 [2048, 1024], P(('lon', 'lat')), may hold values from -0.125 to 0.125
- attend_two: bfloat16 [3, 1024, 1024], P(None, 'lon', 'lat'), may hold values from -1.2 to 1.2
- project_two: bfloat16 [1024, 1024], P('lat', 'lon'), may hold values from -0.1875 to 0.1875
- expand_two: bfloat16 [1024, 4096], P('lon', 'lat'), may hold values from -0.1875 to 0.1875
- reduce_two: bfloat16 [4096, 1024], P('lat', 'lon'), may hold values from -0.09375 to 0.09375
Outputs:
- encoded: bfloat16 [2, 72, 384, 1024], P(None, None, 'lon', 'lat')
The draws below stay inside these ranges and needn't reach their ends.
All inputs are finite; a program needn't handle non-finite values.
Results may differ from the reference program's by a relative error of at most 0.018.
Values may be sent and summed in bfloat16 or wider, within the bound.
A program may use at most 192 MiB of HBM per device.

```python
import jax
import jax.numpy as jnp
from jax import lax

D1 = 512
H1 = 8
F1 = 2048
D2 = 1024
H2 = 16
F2 = 4096
LEV = 2
WLAT = 6
WLON = 12
NLAT = 144
NLON = 768


def draw_attend_one(key, part):
    key = jax.random.fold_in(key, 11)
    first_key = jax.random.fold_in(key, 0)
    drawn = jax.random.normal(first_key, (3, D1, D1), jnp.float32) * D1 ** (-0.5)
    return jnp.clip(drawn, -1.1953125, 1.1953125).astype(jnp.bfloat16)


def draw_attend_two(key, part):
    key = jax.random.fold_in(key, 23)
    first_key = jax.random.fold_in(key, 0)
    drawn = jax.random.normal(first_key, (3, D2, D2), jnp.float32) * D2 ** (-0.5)
    return jnp.clip(drawn, -1.1953125, 1.1953125).astype(jnp.bfloat16)


def touch_ends(drawn, stream_key, low, high):
    longest = drawn.shape.index(max(drawn.shape))
    spots = []
    for shift in (0, 1):
        where = [jax.random.randint(jax.random.fold_in(stream_key, axis), (), 0, length) for axis, length in enumerate(drawn.shape)]
        where[longest] = (where[longest] + shift) % drawn.shape[longest]
        spots.append(tuple(where))
    return drawn.at[spots[0]].set(low).at[spots[1]].set(high)


def shard_levels(key, shape, cuts, low, high):
    loudness, own = 1.0, jax.random.fold_in(key, 6)
    for axis_at, blocks in cuts:
        draws = jnp.exp(jax.random.uniform(jax.random.fold_in(own, axis_at), (blocks,), jnp.float32, low / len(cuts), high / len(cuts)))
        loudness = loudness * jnp.repeat(draws, shape[axis_at] // blocks).reshape([-1 if axis == axis_at else 1 for axis in range(len(shape))])
    return loudness


def noise(key, shape, scale, limit, cuts=(), held_as=jnp.bfloat16):
    loudness = shard_levels(key, shape, cuts, -0.22, 0.18) if cuts else 1.0
    drawn = jax.random.normal(key, shape, jnp.float32) * scale * loudness
    return jnp.minimum(jnp.maximum(drawn, -limit), limit).astype(held_as)


def setup_inputs(seed: int = 0) -> dict:
    seeds = jax.random.split(jax.random.key(seed), 12)
    return {
        "latents": noise(seeds[0], (LEV, NLAT, NLON, D1), 1.0, 6.0, ((1, 4), (2, 32))),
        "region_ids": touch_ends(jax.random.randint(seeds[1], (LEV, NLAT, NLON), 0, 4), jax.random.fold_in(seeds[1], 1), 0, 3).astype(jnp.int32),
        "attend_one": draw_attend_one(jax.random.fold_in(seeds[11], 71), 0),
        "project_one": noise(seeds[3], (D1, D1), D1 ** -0.5, 0.25),
        "expand_one": noise(seeds[4], (D1, F1), D1 ** -0.5, 0.25),
        "reduce_one": noise(seeds[5], (F1, D1), F1 ** -0.5, 0.125),
        "merge_weight": noise(seeds[6], (4 * D1, D2), (4 * D1) ** -0.5, 0.125, ((0, 128),)),
        "attend_two": draw_attend_two(jax.random.fold_in(seeds[11], 71), 0),
        "project_two": noise(seeds[8], (D2, D2), D2 ** -0.5, 0.1875, ((0, 4), (1, 32))),
        "expand_two": noise(seeds[9], (D2, F2), D2 ** -0.5, 0.1875, ((0, 32), (1, 4))),
        "reduce_two": noise(seeds[10], (F2, D2), F2 ** -0.5, 0.09375, ((0, 4), (1, 32))),
    }


EPSILON = 1e-05
MASKED = -1e+30

def layer_norm(values):
    values = values.astype(jnp.float32)
    centered = values - lax.optimization_barrier(jnp.mean(values, axis=-1, keepdims=True))
    variance = lax.optimization_barrier(jnp.mean(centered * centered, axis=-1, keepdims=True))
    return centered / jnp.sqrt(variance + EPSILON)

def to_windows(source, win_lat, win_lon):
    levels, height, extent = (source.shape[0], source.shape[1], source.shape[2])
    trailing = source.shape[3:]
    shaped = source.reshape((levels, height // win_lat, win_lat, extent // win_lon, win_lon) + trailing)
    order = (1, 3, 0, 2, 4) + tuple(range(5, 5 + len(trailing)))
    return shaped.transpose(order).reshape((height // win_lat * (extent // win_lon), levels * win_lat * win_lon) + trailing)

def from_windows(windows, levels, height, extent, win_lat, win_lon):
    trailing = windows.shape[2:]
    shaped = windows.reshape((height // win_lat, extent // win_lon, levels, win_lat, win_lon) + trailing)
    order = (2, 0, 3, 1, 4) + tuple(range(5, 5 + len(trailing)))
    return shaped.transpose(order).reshape((levels, height, extent) + trailing)

def window_attention(packed, region, head_count):
    window_count = packed.shape[0]
    window_len = packed.shape[1]
    channels = packed.shape[3]
    head_size = channels // head_count
    parted = packed.astype(jnp.float32).reshape(window_count, window_len, 3, head_count, head_size)
    scores = jnp.einsum('wqhd,wkhd->whqk', parted[:, :, 0], parted[:, :, 1]) * head_size ** (-0.5)
    if region is not None:
        matching = region[:, :, None] == region[:, None, :]
        scores = jnp.where(matching[:, None], scores, MASKED)
    highest = lax.optimization_barrier(jnp.max(scores, axis=-1, keepdims=True))
    lifted = jnp.exp(scores - highest)
    chances = (lifted / lax.optimization_barrier(jnp.sum(lifted, axis=-1, keepdims=True))).astype(jnp.bfloat16)
    blended = jnp.einsum('whqk,wkhd->wqhd', chances.astype(jnp.float32), parted[:, :, 2])
    return blended.astype(jnp.bfloat16).reshape(window_count, window_len, channels)

def swin_block(source, region, weights, head_count):
    attend, project, expand, shrink = weights
    levels, height, extent, channels = source.shape
    normed = layer_norm(source).astype(jnp.bfloat16)
    packed = jnp.einsum('abci,kio->abcko', normed.astype(jnp.float32), attend.astype(jnp.float32)).astype(jnp.bfloat16)
    region_win = None if region is None else to_windows(region, WLAT, WLON)
    blended = window_attention(to_windows(packed, WLAT, WLON), region_win, head_count)
    blended = from_windows(blended, levels, height, extent, WLAT, WLON).reshape(-1, channels)
    flattened = source.reshape(-1, channels)
    hidden = (flattened.astype(jnp.float32) + jnp.dot(blended, project, preferred_element_type=jnp.float32)).astype(jnp.bfloat16)
    activated = jax.nn.gelu(jnp.dot(layer_norm(hidden).astype(jnp.bfloat16), expand, preferred_element_type=jnp.float32)).astype(jnp.bfloat16)
    result = (hidden.astype(jnp.float32) + jnp.dot(activated, shrink, preferred_element_type=jnp.float32)).astype(jnp.bfloat16)
    return result.reshape(source.shape)

def over_groups(field, region, weights, head_count):
    levels, height, extent, channels = field.shape
    groups = height // WLAT
    stacked = field.reshape(levels, groups, WLAT, extent, channels).transpose(1, 0, 2, 3, 4)
    if region is None:

        def single(strip_in):
            return swin_block(strip_in, None, weights, head_count)
        finished = lax.map(single, stacked)
    else:
        region_rows = region.reshape(levels, groups, WLAT, extent).transpose(1, 0, 2, 3)

        def paired(inputs):
            return swin_block(inputs[0], inputs[1], weights, head_count)
        finished = lax.map(paired, (stacked, region_rows))
    return finished.transpose(1, 0, 2, 3, 4).reshape(levels, height, extent, channels)

def reference(latents, region_ids, attend_one, project_one, expand_one, reduce_one, merge_weight, attend_two, project_two, expand_two, reduce_two):
    half_lat = WLAT // 2
    half_lon = WLON // 2
    rolled = jnp.roll(latents, (-half_lat, -half_lon), axis=(1, 2))
    rolled_ids = jnp.roll(region_ids, (-half_lat, -half_lon), axis=(1, 2))
    section_one = over_groups(rolled, rolled_ids, (attend_one, project_one, expand_one, reduce_one), H1)
    section_one = jnp.roll(section_one, (half_lat, half_lon), axis=(1, 2))
    levels, height, extent, channels = section_one.shape
    quartets = section_one.reshape(levels, height // 2, 2, extent // 2, 2, channels).transpose(0, 1, 3, 4, 2, 5).reshape(-1, 4 * channels)
    merge_input = layer_norm(quartets).astype(jnp.bfloat16)
    merged = jnp.dot(merge_input, merge_weight, preferred_element_type=jnp.float32).astype(jnp.bfloat16)
    merged = merged.reshape(levels, height // 2, extent // 2, merge_weight.shape[1])
    return over_groups(merged, None, (attend_two, project_two, expand_two, reduce_two), H2)
```

```python
import jax
import jax.numpy as jnp
import numpy as np
from jax import lax
from jax.experimental import pallas as pl
from jax.experimental.pallas import tpu as pltpu
from jax.sharding import PartitionSpec as P

MESH = pl.DeviceIdType.MESH
BF = jnp.bfloat16
F32 = jnp.float32
EPSILON = 1e-05
MASKED = -1e30
ORDERS = (("x", "y", "z"), ("y", "z", "x"), ("z", "x", "y"))
WIDTHS = (1280, 1280, 1024)
SUB = (0, -1, 1, 2)


def gather_plan(bufs, send, recv, sibs, sibr):
    lon = lax.axis_index("lon")
    lat = lax.axis_index("lat")
    me = {"x": (lon // 4) % 4, "y": lon % 4, "z": (lon // 16) * 2 + lat // 2}
    core = lat % 2

    def device(pos, c):
        return ((pos["z"] // 2) * 16 + pos["x"] * 4 + pos["y"], (pos["z"] % 2) * 2 + c)

    def shifted(axis, by):
        pos = dict(me)
        pos[axis] = (me[axis] + by + 4) % 4
        return pos

    def part(s, fix, half):
        at = [slice(None) if fix[a] is None else fix[a] for a in ("z", "x", "y")]
        rows = slice(None) if half is None else pl.ds(16 * half, 16)
        return bufs[s].at[core, at[0], at[1], at[2], rows]

    def copy(s, n, fix, axis, by, half=None):
        ref = part(s, fix, half)
        return pltpu.make_async_remote_copy(
            src_ref=ref, dst_ref=ref, send_sem=send.at[s, n], recv_sem=recv.at[s, n],
            device_id=device(shifted(axis, by), core), device_id_type=MESH,
        )

    def sibling(s, k, j):
        ref = part(s, group(s, 3, SUB[k], SUB[j]), None)
        return pltpu.make_async_remote_copy(
            src_ref=ref, dst_ref=ref, send_sem=sibs.at[s, 4 * j + k], recv_sem=sibr.at[s, 4 * j + k],
            device_id=device(me, 1 - core), device_id_type=MESH,
        )

    def group(s, stage, second=0, third=0):
        axes = ORDERS[s]
        fix = dict(me)
        fix[axes[0]] = None
        fix[axes[1]] = (me[axes[1]] + second + 4) % 4
        fix[axes[2]] = (me[axes[2]] + third + 4) % 4
        return fix

    def own(s, by):
        fix = dict(me)
        axis = ORDERS[s][0]
        fix[axis] = (me[axis] + by + 4) % 4
        return fix

    def first(s):
        a = ORDERS[s][0]
        return copy(s, 0, own(s, 0), a, 1), copy(s, 1, own(s, 0), a, -1)

    def first_on(s):
        a = ORDERS[s][0]
        return copy(s, 2, own(s, -1), a, 1, 0), copy(s, 3, own(s, 1), a, -1, 1)

    def second(s):
        a = ORDERS[s][1]
        return copy(s, 4, group(s, 2), a, 1), copy(s, 5, group(s, 2), a, -1)

    def second_on(s):
        a = ORDERS[s][1]
        return copy(s, 6, group(s, 2, -1), a, 1, 0), copy(s, 7, group(s, 2, 1), a, -1, 1)

    def third(s, k):
        a = ORDERS[s][2]
        fix = group(s, 3, SUB[k])
        return copy(s, 8 + 4 * k, fix, a, 1), copy(s, 9 + 4 * k, fix, a, -1)

    def third_on(s, k):
        a = ORDERS[s][2]
        return (
            copy(s, 10 + 4 * k, group(s, 3, SUB[k], -1), a, 1, 0),
            copy(s, 11 + 4 * k, group(s, 3, SUB[k], 1), a, -1, 1),
        )

    def go(copies):
        for c in copies:
            c.start()

    def got(copies):
        for c in copies:
            c.wait_recv()

    streams = range(3)

    def e0():
        for s in streams:
            go(first(s))

    def e1():
        for s in streams:
            got(first(s))
            go(first_on(s))

    def e2():
        for s in streams:
            got(first_on(s))
            go(second(s))
            go(third(s, 0))
        for s in streams:
            sibling(s, 0, 0).start()

    def e3():
        for s in streams:
            got(second(s))
            go(second_on(s))
            go(third(s, 1))
            go(third(s, 2))
        for s in streams:
            sibling(s, 1, 0).start()
            sibling(s, 2, 0).start()
        for s in streams:
            got(third(s, 0))
            go(third_on(s, 0))
            sibling(s, 0, 1).start()
            sibling(s, 0, 2).start()

    def e4():
        for s in streams:
            got(second_on(s))
            go(third(s, 3))
            sibling(s, 3, 0).start()
        for k in (1, 2):
            for s in streams:
                got(third(s, k))
                go(third_on(s, k))
                sibling(s, k, 1).start()
                sibling(s, k, 2).start()

    def e5():
        for s in streams:
            got(third_on(s, 0))
            sibling(s, 0, 3).start()
        for s in streams:
            got(third(s, 3))
            go(third_on(s, 3))
            sibling(s, 3, 1).start()
            sibling(s, 3, 2).start()

    def e6():
        for k in (1, 2):
            for s in streams:
                got(third_on(s, k))
                sibling(s, k, 3).start()

    def e7():
        for s in streams:
            got(third_on(s, 3))
            sibling(s, 3, 3).start()

    def arrived(s):
        for j in range(4):
            for k in range(4):
                sibling(s, k, j).wait_recv()

    def drain():
        for s in streams:
            for c in first(s) + first_on(s) + second(s) + second_on(s):
                c.wait_send()
            for k in range(4):
                for c in third(s, k) + third_on(s, k):
                    c.wait_send()
                for j in range(4):
                    sibling(s, k, j).wait_send()

    partners = [device(shifted(a, d), core) for a in "xyz" for d in (1, -1)] + [device(me, 1 - core)]
    return me, core, (e0, e1, e2, e3, e4, e5, e6, e7), arrived, drain, partners


def normed(values):
    centered = values - jnp.mean(values, axis=-1, keepdims=True)
    variance = jnp.mean(centered * centered, axis=-1, keepdims=True)
    return centered * lax.rsqrt(variance + EPSILON)


def gelu(v):
    return 0.5 * v * (1.0 + jnp.tanh(0.7978845608028654 * (v + 0.044715 * (v * v * v))))


def mm(a, b):
    return jnp.dot(a, b, preferred_element_type=F32)


def mm_nt(a, b):
    return lax.dot_general(a, b, (((1,), (1,)), ((), ())), preferred_element_type=F32)


def attend_heads(q, k, v, bias):
    lane = lax.broadcasted_iota(jnp.int32, q.shape, 1)
    low_f = (lane < 64).astype(F32)
    low = low_f.astype(BF)
    high = (1.0 - low_f).astype(BF)

    def weights(keys):
        s = mm_nt(q, keys)
        if bias is not None:
            s = s + bias
        return jnp.exp(s - jnp.max(s, axis=-1, keepdims=True)).astype(BF)

    even = mm(weights(k * low), v * low + high)
    odd = mm(weights(k * high), v * high + low)
    is_low = lane < 64
    total = jnp.where(is_low, odd, even)
    return (jnp.where(is_low, even, odd) / pltpu.roll(total, 64, 1)).astype(BF)


def kernel(
    tile, reg_row, reg_col, attend, project, expand, shrink,
    pick_row, pick_col, put, quart_row, quart_col, mix, pad,
    in0, in1, in2,
    out,
    b0, b1, b2, rows, cols, y_rows, y_east, y_west, quart, merged, qkv, blend, hidden, norm2, total, result,
    send, recv, sibs, sibr, loc, halo_s, halo_r, back_s, back_r, fin_s, fin_r,
):
    bufs = (b0, b1, b2)
    me, core, events, arrived, drain, partners = gather_plan(bufs, send, recv, sibs, sibr)
    lon = lax.axis_index("lon")
    lat = lax.axis_index("lat")
    west, east = (lon + 31) % 32, (lon + 1) % 32
    above, below = (lat + 3) % 4, (lat + 1) % 4

    local = [
        pltpu.make_async_copy(src, b.at[core, me["z"], me["x"], me["y"]], loc.at[n])
        for n, (src, b) in enumerate(zip((in0, in1, in2), bufs))
    ]
    local.append(pltpu.make_async_copy(tile, rows.at[pl.ds(0, 36)], loc.at[3]))
    for c in local:
        c.start()
    everyone = partners + [(west, lat), (east, lat), (lon, above), (lon, below), (lon, (lat + 2) % 4)]
    everyone += [(west, above), (east, below)]
    barrier = pltpu.get_barrier_semaphore()
    for d in everyone:
        pl.semaphore_signal(barrier, inc=1, device_id=d, device_id_type=MESH)
    pl.semaphore_wait(barrier, len(everyone))

    def remote(src, dst, ssem, rsem, to):
        return pltpu.make_async_remote_copy(
            src_ref=src, dst_ref=dst, send_sem=ssem, recv_sem=rsem, device_id=to, device_id_type=MESH
        )

    halos = [
        remote(tile.at[:, pl.ds(0, 16)], cols.at[pl.ds(0, 36)], halo_s.at[0], halo_r.at[0], (west, lat)),
        remote(tile.at[pl.ds(0, 3)], rows.at[pl.ds(36, 3)], halo_s.at[1], halo_r.at[1], (lon, above)),
        remote(tile.at[pl.ds(0, 3), pl.ds(0, 16)], cols.at[pl.ds(36, 3)], halo_s.at[2], halo_r.at[2], (west, above)),
    ]
    for c in halos:
        c.start()
    for c in local:
        c.wait()
    events[0]()
    for c in halos:
        c.wait_recv()

    def to_east(a):
        span = pl.ds(6 * a + 3, 6)
        return remote(y_east.at[span], y_west.at[span], back_s.at[a], back_r.at[a], (east, lat))

    edge = [
        remote(y_east.at[pl.ds(33, 3)], y_west.at[pl.ds(33, 3)], back_s.at[5], back_r.at[5], (east, lat)),
        remote(y_east.at[pl.ds(36, 3)], y_west.at[pl.ds(0, 3)], back_s.at[6], back_r.at[6], (east, below)),
        remote(y_rows.at[pl.ds(36, 3)], y_rows.at[pl.ds(0, 3)], back_s.at[7], back_r.at[7], (lon, below)),
    ]

    def pair(t, carry):
        a = lax.rem(t + 5, 6)
        span = pl.ds(6 * a + 3, 6)
        own = rows[span].reshape(288, 512)
        side = cols[span].reshape(96, 512)
        x = mm(pick_row[...], own) + mm(pick_col[...], side)
        n = normed(x).astype(BF)
        q = (mm(n, attend[0]) * 0.125).astype(BF)
        k = mm(n, attend[1]).astype(BF)
        v = mm(n, attend[2]).astype(BF)
        parts = []
        for b in range(2):
            same = reg_col[2 * a + b] == reg_row[2 * a + b]
            bias = jnp.where(same, 0.0, MASKED)
            r = slice(144 * b, 144 * b + 144)
            heads = [
                attend_heads(q[r, 128 * h : 128 * h + 128], k[r, 128 * h : 128 * h + 128], v[r, 128 * h : 128 * h + 128], bias)
                for h in range(4)
            ]
            parts.append(jnp.concatenate(heads, axis=1))
        o = jnp.concatenate(parts, axis=0)

        @pl.when(t == 0)
        def _():
            events[1]()

        hid = (x + mm(o, project[...])).astype(BF)
        hid_f = hid.astype(F32)
        n = normed(hid_f).astype(BF)
        acc = hid_f
        for c in range(4):
            u = gelu(mm(n, expand[:, 512 * c : 512 * c + 512])).astype(BF)
            acc = acc + mm(u, shrink[512 * c : 512 * c + 512, :])
        placed = mm(put[...], acc.astype(BF)).astype(BF)
        y_rows[span] = placed[:288].reshape(6, 48, 512)
        y_east[span] = placed[288:].reshape(6, 16, 512)

        @pl.when(t == 0)
        def _():
            for c in edge:
                c.start()

        @pl.when(t > 0)
        def _():
            to_east(a).start()

        for at, event in ((0, 2), (1, 3), (3, 4), (4, 5), (5, 6)):

            @pl.when(t == at)
            def _(event=event):
                events[event]()

        return carry

    lax.fori_loop(0, 6, pair, 0)
    events[7]()

    for c in edge:
        c.wait_recv()
    for a in range(5):
        to_east(a).wait_recv()

    for w in range(3):
        span = pl.ds(12 * w, 12)
        both = y_rows[span].reshape(6, 2, 48, 512)
        side = y_west[span].reshape(6, 2, 16, 512)
        found = []
        for odd in range(2):
            got = mm(quart_row[...], both[:, odd].reshape(288, 512)) + mm(quart_col[...], side[:, odd].reshape(96, 512))
            found.append(got)
        quads = [found[0][:144], found[1][:144], found[0][144:], found[1][144:]]
        mean = sum(jnp.sum(p, axis=-1, keepdims=True) for p in quads) * (1.0 / 2048.0)
        quads = [p - mean for p in quads]
        variance = sum(jnp.sum(p * p, axis=-1, keepdims=True) for p in quads) * (1.0 / 2048.0)
        scale = lax.rsqrt(variance + EPSILON)
        for p in range(4):
            quart[p, pl.ds(144 * w, 144)] = mm((quads[p] * scale).astype(BF), mix[...]).astype(BF)

    arrived(0)
    for half in range(2):
        acc = jnp.zeros((432, 512), F32)
        for z in range(4):
            for c in range(2):
                ch = slice(128 * ((z % 2) * 2 + c), 128 * ((z % 2) * 2 + c) + 128)
                left = jnp.concatenate([quart[z // 2 * 2, :, ch], quart[z // 2 * 2 + 1, :, ch]], axis=1)
                right = b0[c, z, :, :, pl.ds(16 * half, 16), pl.ds(768, 512)].reshape(256, 512)
                acc = acc + mm(left, right)
        merged[:, pl.ds(512 * half, 512)] = acc.astype(BF)

    norm2[...] = normed(merged[...].astype(F32)).astype(BF)

    def attend_slice(g, carry):
        z_lo, c = g // 2, g % 2
        acc = mm(norm2[:, pl.ds(0, 512)], b0[c, z_lo, :, :, :, pl.ds(0, 768)].reshape(512, 768))
        acc = acc + mm(norm2[:, pl.ds(512, 512)], b0[c, z_lo + 2, :, :, :, pl.ds(0, 768)].reshape(512, 768))
        q = (acc[:, :256] * 0.125).astype(BF)
        qkv[:, pl.ds(0, 256)] = q
        qkv[:, pl.ds(256, 512)] = acc[:, 256:].astype(BF)
        for w in range(3):
            r = pl.ds(144 * w, 144)
            for h in range(2):
                blend[g, r, pl.ds(128 * h, 128)] = attend_heads(
                    qkv[r, pl.ds(128 * h, 128)], qkv[r, pl.ds(256 + 128 * h, 128)], qkv[r, pl.ds(512 + 128 * h, 128)], None
                )
        return carry

    lax.fori_loop(0, 4, attend_slice, 0)

    arrived(1)
    for half in range(2):
        acc = merged[:, pl.ds(512 * half, 512)].astype(F32)
        for g in range(4):
            w_t = b1[g % 2, 2 * half + g // 2, :, :, :, pl.ds(1024, 256)].reshape(512, 256)
            acc = acc + mm_nt(blend[g], w_t)
        hidden[:, pl.ds(512 * half, 512)] = acc.astype(BF)
    total[...] = hidden[...].astype(F32)
    norm2[...] = normed(total[...]).astype(BF)
    arrived(2)

    def feed(g, carry):
        z_lo, c = g // 2, g % 2
        u = mm(norm2[:, pl.ds(0, 512)], b1[c, z_lo, :, :, :, pl.ds(0, 1024)].reshape(512, 1024))
        u = u + mm(norm2[:, pl.ds(512, 512)], b1[c, z_lo + 2, :, :, :, pl.ds(0, 1024)].reshape(512, 1024))
        u = gelu(u).astype(BF)
        for half in range(2):
            h = pl.ds(512 * half, 512)
            total[:, h] += mm_nt(u, b2[c, z_lo + 2 * half].reshape(512, 1024))
        return carry

    lax.fori_loop(0, 4, feed, 0)

    for w in range(3):
        spread = mm(pad[...], total[pl.ds(144 * w, 144)].astype(BF)).astype(BF).reshape(12, 16, 1024)
        for p in range(4):
            for level in range(2):
                result[p, level, pl.ds(6 * w, 6)] = spread[6 * level : 6 * level + 6, :12, 256 * p : 256 * p + 256]

    mine = out.at[:, pl.ds(18 * lat, 18)]
    keep = pltpu.make_async_copy(result.at[lat], mine, loc.at[4])
    last = [remote(result.at[(lat + d) % 4], mine, fin_s.at[d - 1], fin_r.at[d - 1], (lon, (lat + d) % 4)) for d in (1, 2, 3)]
    for c in last:
        c.start()
    keep.start()
    keep.wait()
    for c in last:
        c.wait()
    drain()
    for c in halos + edge + [to_east(a) for a in range(5)]:
        c.wait_send()


def choose(shape, pairs):
    out = np.zeros(shape, np.float32)
    for r, c in pairs:
        out[r, c] = 1.0
    return jnp.asarray(out, BF)


def choices():
    row, col, put_to, qrow, qcol = [], [], [], [], []
    for b in range(2):
        for rho in range(6):
            for hh in range(2):
                for lc in range(12):
                    i = b * 144 + rho * 24 + hh * 12 + lc
                    h = 1 + 2 * b + hh
                    if h < 4:
                        row.append((i, rho * 48 + h * 12 + lc))
                        put_to.append((rho * 48 + (h - 1) * 12 + lc, i))
                    else:
                        col.append((i, rho * 16 + lc))
                        put_to.append((288 + rho * 16 + lc, i))
    for pc in range(2):
        for level in range(2):
            for ii in range(6):
                for j in range(12):
                    i = pc * 144 + level * 72 + ii * 12 + j
                    h, c = divmod(2 * j + pc, 6)
                    if h:
                        qrow.append((i, ii * 48 + (h - 1) * 12 + level * 6 + c))
                    else:
                        qcol.append((i, ii * 16 + level * 6 + c))
    mix = [(blk * 64 + g * 16 + r, g * 128 + blk * 16 + r) for g in range(4) for blk in range(8) for r in range(16)]
    pad = [(g * 16 + j, g * 12 + j) for g in range(12) for j in range(12)]
    return (
        choose((288, 288), row), choose((288, 96), col), choose((384, 288), put_to),
        choose((288, 288), qrow), choose((288, 96), qcol), choose((512, 512), mix), choose((192, 144), pad),
    )


def window_ids(region_ids):
    lat = lax.axis_index("lat")
    lon = lax.axis_index("lon")

    def rows_of(col, width):
        own = lax.dynamic_slice(region_ids, (0, lat * 36, col), (2, 36, width))
        under = lax.dynamic_slice(region_ids, (0, (lat + 1) % 4 * 36, col), (2, 3, width))
        return jnp.concatenate([own[:, 3:], under], axis=1)

    ids = jnp.concatenate([rows_of(lon * 24, 24)[:, :, 6:], rows_of((lon + 1) % 32 * 24, 6)], axis=2)
    ids = ids.reshape(2, 6, 6, 2, 2, 6).transpose(1, 3, 2, 4, 0, 5).reshape(12, 144)
    return ids[:, None, :], ids[:, :, None]


def body(
    latents, region_ids, attend_one, project_one, expand_one, reduce_one,
    merge_weight, attend_two, project_two, expand_two, reduce_two,
):
    tile = latents.reshape(2, 36, 4, 6, 512).transpose(1, 2, 0, 3, 4).reshape(36, 48, 512)
    reg_row, reg_col = window_ids(region_ids)
    in0 = jnp.concatenate(
        [attend_two.transpose(1, 0, 2).reshape(32, 768), jnp.concatenate([merge_weight[:, :512], merge_weight[:, 512:]], axis=0)],
        axis=1,
    )
    in1 = jnp.concatenate([expand_two, project_two.T], axis=1)
    in2 = reduce_two.T
    vmem = pl.BlockSpec(memory_space=pltpu.VMEM)
    hbm = pl.BlockSpec(memory_space=pl.ANY)
    sem = pltpu.SemaphoreType.DMA
    return pl.pallas_call(
        kernel,
        out_shape=jax.ShapeDtypeStruct((2, 72, 12, 256), BF),
        in_specs=[hbm] + [vmem] * 13 + [hbm] * 3,
        out_specs=hbm,
        scratch_shapes=[pltpu.VMEM((2, 4, 4, 4, 32, w), BF) for w in WIDTHS]
        + [
            pltpu.VMEM((39, 48, 512), BF), pltpu.VMEM((39, 16, 512), BF),
            pltpu.VMEM((39, 48, 512), BF), pltpu.VMEM((39, 16, 512), BF), pltpu.VMEM((36, 16, 512), BF),
            pltpu.VMEM((4, 432, 512), BF), pltpu.VMEM((432, 1024), BF), pltpu.VMEM((432, 768), BF),
            pltpu.VMEM((4, 432, 256), BF), pltpu.VMEM((432, 1024), BF), pltpu.VMEM((432, 1024), BF),
            pltpu.VMEM((432, 1024), F32), pltpu.VMEM((4, 2, 18, 12, 256), BF),
            sem((3, 24)), sem((3, 24)), sem((3, 16)), sem((3, 16)), sem((5,)),
            sem((3,)), sem((3,)), sem((8,)), sem((8,)), sem((3,)), sem((3,)),
        ],
        compiler_params=pltpu.CompilerParams(collective_id=0, has_side_effects=True, vmem_limit_bytes=63 * 2**20),
        cost_estimate=pl.CostEstimate(flops=24 * 10**9, bytes_accessed=10 * 10**6, transcendentals=10**7),
    )(
        tile, reg_row, reg_col, attend_one, project_one, expand_one, reduce_one, *choices(), in0, in1, in2
    )


def solution(mesh):
    return jax.shard_map(
        body,
        mesh=mesh,
        in_specs=(
            P(None, "lat", "lon", None), P(), P(), P(), P(), P(),
            P(("lon", "lat"), None), P(None, "lon", "lat"), P("lat", "lon"), P("lon", "lat"), P("lat", "lon"),
        ),
        out_specs=P(None, None, "lon", "lat"),
        check_vma=False,
    )
```

```python
import jax
import jax.numpy as jnp
import numpy as np
from jax import lax
from jax.experimental import pallas as pl
from jax.experimental.pallas import tpu as pltpu
from jax.sharding import PartitionSpec as P

MESH = pl.DeviceIdType.MESH
BF = jnp.bfloat16
F32 = jnp.float32
EPSILON = 1e-05
MASKED = -1e30
ORDERS = (("x", "y", "z"), ("y", "z", "x"), ("z", "x", "y"))
WIDTHS = (1280, 2304)
SPANS = (((0, 384), (384, 512), (896, 384)), ((0, 640), (640, 768), (1408, 896)))
SUB = (0, -1, 1, 2)


def gather_plan(kind, buf, send, recv, sibs, sibr):
    lon = lax.axis_index("lon")
    lat = lax.axis_index("lat")
    me = {"x": (lon // 4) % 4, "y": lon % 4, "z": (lon // 16) * 2 + lat // 2}
    core = lat % 2

    def device(pos, c):
        return ((pos["z"] // 2) * 16 + pos["x"] * 4 + pos["y"], (pos["z"] % 2) * 2 + c)

    def shifted(axis, by):
        pos = dict(me)
        pos[axis] = (me[axis] + by + 4) % 4
        return pos

    def part(s, fix, half):
        at = [slice(None) if fix[a] is None else fix[a] for a in ("z", "x", "y")]
        rows = slice(None) if half is None else pl.ds(16 * half, 16)
        return buf.at[core, at[0], at[1], at[2], rows, pl.ds(*SPANS[kind][s])]

    def copy(s, n, fix, axis, by, half=None):
        ref = part(s, fix, half)
        return pltpu.make_async_remote_copy(
            src_ref=ref, dst_ref=ref, send_sem=send.at[3 * kind + s, n], recv_sem=recv.at[3 * kind + s, n],
            device_id=device(shifted(axis, by), core), device_id_type=MESH,
        )

    def sibling(s, k, j):
        ref = part(s, group(s, 3, SUB[k], SUB[j]), None)
        return pltpu.make_async_remote_copy(
            src_ref=ref, dst_ref=ref, send_sem=sibs.at[3 * kind + s, 4 * j + k], recv_sem=sibr.at[3 * kind + s, 4 * j + k],
            device_id=device(me, 1 - core), device_id_type=MESH,
        )

    def group(s, stage, second=0, third=0):
        axes = ORDERS[s]
        fix = dict(me)
        fix[axes[0]] = None
        fix[axes[1]] = (me[axes[1]] + second + 4) % 4
        fix[axes[2]] = (me[axes[2]] + third + 4) % 4
        return fix

    def own(s, by):
        fix = dict(me)
        axis = ORDERS[s][0]
        fix[axis] = (me[axis] + by + 4) % 4
        return fix

    def first(s):
        a = ORDERS[s][0]
        return copy(s, 0, own(s, 0), a, 1), copy(s, 1, own(s, 0), a, -1)

    def first_on(s):
        a = ORDERS[s][0]
        return copy(s, 2, own(s, -1), a, 1, 0), copy(s, 3, own(s, 1), a, -1, 1)

    def second(s):
        a = ORDERS[s][1]
        return copy(s, 4, group(s, 2), a, 1), copy(s, 5, group(s, 2), a, -1)

    def second_on(s):
        a = ORDERS[s][1]
        return copy(s, 6, group(s, 2, -1), a, 1, 0), copy(s, 7, group(s, 2, 1), a, -1, 1)

    def third(s, k):
        a = ORDERS[s][2]
        fix = group(s, 3, SUB[k])
        return copy(s, 8 + 4 * k, fix, a, 1), copy(s, 9 + 4 * k, fix, a, -1)

    def third_on(s, k):
        a = ORDERS[s][2]
        return (
            copy(s, 10 + 4 * k, group(s, 3, SUB[k], -1), a, 1, 0),
            copy(s, 11 + 4 * k, group(s, 3, SUB[k], 1), a, -1, 1),
        )

    def go(copies):
        for c in copies:
            c.start()

    def got(copies):
        for c in copies:
            c.wait_recv()

    streams = range(3)

    def e0():
        for s in streams:
            go(first(s))

    def e1():
        for s in streams:
            got(first(s))
            go(first_on(s))

    def e2():
        for s in streams:
            got(first_on(s))
            go(second(s))
            go(third(s, 0))
        for s in streams:
            sibling(s, 0, 0).start()

    def e3():
        for s in streams:
            got(second(s))
            go(second_on(s))
            go(third(s, 1))
            go(third(s, 2))
        for s in streams:
            sibling(s, 1, 0).start()
            sibling(s, 2, 0).start()
        for s in streams:
            got(third(s, 0))
            go(third_on(s, 0))
            sibling(s, 0, 1).start()
            sibling(s, 0, 2).start()

    def e4():
        for s in streams:
            got(second_on(s))
            go(third(s, 3))
            sibling(s, 3, 0).start()
        for k in (1, 2):
            for s in streams:
                got(third(s, k))
                go(third_on(s, k))
                sibling(s, k, 1).start()
                sibling(s, k, 2).start()

    def e5():
        for s in streams:
            got(third_on(s, 0))
            sibling(s, 0, 3).start()
        for s in streams:
            got(third(s, 3))
            go(third_on(s, 3))
            sibling(s, 3, 1).start()
            sibling(s, 3, 2).start()

    def e6():
        for k in (1, 2):
            for s in streams:
                got(third_on(s, k))
                sibling(s, k, 3).start()

    def e7():
        for s in streams:
            got(third_on(s, 3))
            sibling(s, 3, 3).start()

    def arrived(which):
        for j in range(4):
            for k in range(4):
                for s in which:
                    sibling(s, k, j).wait_recv()

    def drain():
        for s in streams:
            for c in first(s) + first_on(s) + second(s) + second_on(s):
                c.wait_send()
            for k in range(4):
                for c in third(s, k) + third_on(s, k):
                    c.wait_send()
                for j in range(4):
                    sibling(s, k, j).wait_send()

    partners = [device(shifted(a, d), core) for a in "xyz" for d in (1, -1)] + [device(me, 1 - core)]
    return me, core, (e0, e1, e2, e3, e4, e5, e6, e7), arrived, drain, partners


def normed(values):
    centered = values - jnp.mean(values, axis=-1, keepdims=True)
    variance = jnp.mean(centered * centered, axis=-1, keepdims=True)
    return centered * lax.rsqrt(variance + EPSILON)


def gelu(v):
    return 0.5 * v * (1.0 + jnp.tanh(0.7978845608028654 * (v + 0.044715 * (v * v * v))))


def mm(a, b):
    return jnp.dot(a, b, preferred_element_type=F32)


def mm_nt(a, b):
    return lax.dot_general(a, b, (((1,), (1,)), ((), ())), preferred_element_type=F32)


def attend_heads(pairs):
    is_low = lax.broadcasted_iota(jnp.int32, pairs[0][0].shape, 1) < 64
    low_f = (lax.broadcasted_iota(jnp.int32, pairs[0][1].shape, 1) < 64).astype(F32)
    low = low_f.astype(BF)
    high = (1.0 - low_f).astype(BF)
    scores = []
    for q, k, _, bias in pairs:
        for mask in (low, high):
            s = mm_nt(q, k * mask)
            scores.append(s if bias is None else s + bias)
    highest = [jnp.max(s, axis=-1, keepdims=True) for s in scores]
    lifted = [jnp.exp(s - m).astype(BF) for s, m in zip(scores, highest)]
    blends = []
    for n, (_, _, v, _) in enumerate(pairs):
        blends.append((mm(lifted[2 * n], v * low + high), mm(lifted[2 * n + 1], v * high + low)))
    outs = []
    for even, odd in blends:
        sums = pltpu.roll(jnp.where(is_low, odd, even), 64, 1)
        outs.append(jnp.where(is_low, even, odd) / sums)
    return outs


def kernel(
    latents, ids, attend_h, project_h, expand_h, shrink_h, merge_h, attend2_h, project2_h, expand2_h, reduce2_h,
    pick_own_h, pick_side_h, put_h, quarter_h, mix_h, pad_h,
    out,
    b0, b1, tile, edge_w, edge_e, cols_w, cols_e, y_rows, quart, merged, qkv, blend, norm2, total, lifted, result,
    attend, project, expand, shrink, pick_own, pick_side, put, quarter, mix, pad,
    send, recv, sibs, sibr, loc, wsem, halo_s, halo_r, fin_s, fin_r,
):
    me, core, first_events, first_arrived, first_drain, partners = gather_plan(0, b0, send, recv, sibs, sibr)
    _, _, later_events, later_arrived, later_drain, _ = gather_plan(1, b1, send, recv, sibs, sibr)
    lon = lax.axis_index("lon")
    lat = lax.axis_index("lat")
    west, east = (lon + 31) % 32, (lon + 1) % 32
    above, below = (lat + 3) % 4, (lat + 1) % 4

    fetch_tile = pltpu.make_async_copy(latents, tile.at[:, pl.ds(3, 36)], loc.at[0])
    fetch_tile.start()
    at = (core, me["z"], me["x"], me["y"])
    shards = [
        (merge_h.at[:, pl.ds(0, 512)], b0.at[at + (pl.ds(0, 16), pl.ds(768, 512))]),
        (merge_h.at[:, pl.ds(512, 512)], b0.at[at + (pl.ds(16, 16), pl.ds(768, 512))]),
    ]
    shards += [(attend2_h.at[i], b0.at[at + (slice(None), pl.ds(256 * i, 256))]) for i in range(3)]
    shards += [
        (project2_h, b1.at[at + (slice(None), pl.ds(0, 256))]),
        (expand2_h, b1.at[at + (slice(None), pl.ds(256, 1024))]),
        (reduce2_h, b1.at[at + (slice(None), pl.ds(1280, 1024))]),
    ]
    shards = [pltpu.make_async_copy(src, dst, loc.at[n + 1]) for n, (src, dst) in enumerate(shards)]
    for c in shards:
        c.start()
    weights = [
        pltpu.make_async_copy(src, dst, wsem.at[n])
        for n, (src, dst) in enumerate(
            (
                (pick_own_h, pick_own), (pick_side_h, pick_side), (attend_h, attend), (project_h, project), (expand_h, expand),
                (shrink_h, shrink), (put_h, put), (quarter_h, quarter), (mix_h, mix), (pad_h, pad),
            )
        )
    ]
    for c in weights:
        c.start()
    everyone = partners + [(west, lat), (east, lat), (lon, above), (lon, below), (lon, (lat + 2) % 4)]
    everyone += [(west, above), (east, below), (west, below), (east, above)]
    barrier = pltpu.get_barrier_semaphore()
    for d in everyone:
        pl.semaphore_signal(barrier, inc=1, device_id=d, device_id_type=MESH)
    fetch_tile.wait()
    for level in range(2):
        edge_w[:, pl.ds(8 * level, 8)] = tile[level, pl.ds(3, 36), pl.ds(0, 8)]
        edge_e[:, pl.ds(8 * level, 8)] = tile[level, pl.ds(3, 36), pl.ds(16, 8)]
    for c in shards:
        c.wait()
    pl.semaphore_wait(barrier, len(everyone))

    def remote(src, dst, ssem, rsem, to):
        return pltpu.make_async_remote_copy(
            src_ref=src, dst_ref=dst, send_sem=ssem, recv_sem=rsem, device_id=to, device_id_type=MESH
        )

    def halo(n, src, dst, to):
        return remote(src, dst, halo_s.at[n], halo_r.at[n], to)

    def sides(a):
        here, there = pl.ds(6 * a - 3, 6), pl.ds(6 * a, 6)
        return [
            halo(2 * a - 2, edge_w.at[here], cols_e.at[there], (west, lat)),
            halo(2 * a - 1, edge_e.at[here], cols_w.at[there], (east, lat)),
        ]

    top, low = pl.ds(0, 3), pl.ds(33, 3)
    before, after = pl.ds(0, 3), pl.ds(39, 3)
    rim = [
        halo(10, edge_w.at[top], cols_e.at[pl.ds(3, 3)], (west, lat)),
        halo(11, edge_e.at[top], cols_w.at[pl.ds(3, 3)], (east, lat)),
        halo(12, edge_w.at[low], cols_e.at[pl.ds(36, 3)], (west, lat)),
        halo(13, edge_e.at[low], cols_w.at[pl.ds(36, 3)], (east, lat)),
        halo(14, edge_w.at[top], cols_e.at[after], (west, above)),
        halo(15, edge_e.at[top], cols_w.at[after], (east, above)),
        halo(16, edge_w.at[low], cols_e.at[before], (west, below)),
        halo(17, edge_e.at[low], cols_w.at[before], (east, below)),
        halo(18, latents.at[:, top], tile.at[:, after], (lon, above)),
        halo(19, latents.at[:, low], tile.at[:, before], (lon, below)),
    ]
    first_events[0]()
    for a in (1, 2):
        for c in sides(a):
            c.start()
    later_events[0]()
    for c in sides(3):
        c.start()
    for c in weights:
        c.wait()

    early = {
        (0, 0): (first_events[1], later_events[1]), (0, 2): (first_events[2],),
        (1, 1): (first_events[3],), (1, 2): (later_events[2],),
        (2, 1): (first_events[4],), (2, 2): (later_events[3],),
        (3, 1): (first_events[5],), (3, 2): (first_events[6],),
        (4, 0): (later_events[4],), (4, 1): (first_events[7],), (5, 1): (later_events[5],),
    }

    def step_events(t, half):
        for (when, which), events in early.items():
            if which == half:

                @pl.when(t == when)
                def _(events=events):
                    for event in events:
                        event()

    def strip(t, carry):
        a = jnp.where(t < 5, t + 1, (t - 5) * 6)

        @pl.when(t < 5)
        def _():
            for c in sides(t + 1):
                c.wait_recv()

        @pl.when(t == 5)
        def _():
            for c in rim:
                c.wait_recv()

        span = pl.ds(6 * a, 6)
        own = tile[:, span].astype(F32).reshape(288, 512).astype(BF)
        side = jnp.concatenate([cols_w[span].reshape(96, 512), cols_e[span].reshape(96, 512)], axis=0)
        x = mm(pick_own[...], own) + mm(pick_side[...], side)
        n = normed(x).astype(BF)
        q = (mm(n[:360], attend[0]) * 0.125).astype(BF)
        k = mm(n, attend[1]).astype(BF)
        v = mm(n, attend[2]).astype(BF)
        parts = []
        for b, size in enumerate((72, 144, 72)):
            kinds = lax.broadcasted_iota(jnp.int32, (16, 144), 0)
            hot = (ids[pl.ds(3 * a + b, 1), :] == kinds).astype(F32).astype(BF)
            same = lax.dot_general(hot, hot, (((0,), (0,)), ((), ())), preferred_element_type=F32)
            bias = ((same - 1.0) * -MASKED)[:size]
            r = slice(144 * b, 144 * b + 144)
            r_q = slice(144 * b, 144 * b + size)
            heads = [(q[r_q, c : c + 128], k[r, c : c + 128], v[r, c : c + 128], bias) for c in range(0, 512, 128)]
            parts.append(jnp.concatenate(attend_heads(heads), axis=1))
        o = jnp.concatenate(parts, axis=0).astype(BF)
        x = jnp.concatenate([x[:72], x[144:360]], axis=0)
        step_events(t, 0)
        for when in range(2):

            @pl.when(t == when)
            def _(when=when):
                for c in sides(when + 4):
                    c.start()

        @pl.when(t == 2)
        def _():
            for c in rim:
                c.start()

        hid = (x + mm(o, project[...])).astype(BF)
        hid_f = hid.astype(F32)
        n = normed(hid_f).astype(BF)
        acc = hid_f
        for c in range(4):
            u = gelu(mm(n, expand[:, 512 * c : 512 * c + 512])).astype(BF)
            acc = acc + mm(u, shrink[512 * c : 512 * c + 512, :])
            if c == 1:
                step_events(t, 1)
        y_rows[span] = mm(put[...], acc.astype(BF)).astype(BF).reshape(6, 48, 512)
        step_events(t, 2)
        return carry

    lax.fori_loop(0, 7, strip, 0)

    for w in range(3):
        both = y_rows[pl.ds(12 * w + 3, 12)].reshape(6, 2, 48, 512)
        found = [mm(quarter[...], both[:, odd].reshape(288, 512)) for odd in range(2)]
        quads = [found[0][:144], found[1][:144], found[0][144:], found[1][144:]]
        mean = sum(jnp.sum(p, axis=-1, keepdims=True) for p in quads) * (1.0 / 2048.0)
        quads = [p - mean for p in quads]
        variance = sum(jnp.sum(p * p, axis=-1, keepdims=True) for p in quads) * (1.0 / 2048.0)
        scale = lax.rsqrt(variance + EPSILON)
        for p in range(4):
            quart[p, pl.ds(144 * w, 144)] = mm((quads[p] * scale).astype(BF), mix[...]).astype(BF)

    later_events[6]()
    first_arrived(range(3))
    for half in range(2):
        acc = jnp.zeros((432, 512), F32)
        for z in range(4):
            for c in range(2):
                ch = slice(128 * ((z % 2) * 2 + c), 128 * ((z % 2) * 2 + c) + 128)
                left = jnp.concatenate([quart[z // 2 * 2, :, ch], quart[z // 2 * 2 + 1, :, ch]], axis=1)
                right = b0[c, z, :, :, pl.ds(16 * half, 16), pl.ds(768, 512)].reshape(256, 512)
                acc = acc + mm(left, right)
        merged[:, pl.ds(512 * half, 512)] = acc.astype(BF)

    norm2[...] = normed(merged[...].astype(F32)).astype(BF)

    def attend_slice(g, carry):
        z_lo, c = g // 2, g % 2
        acc = mm(norm2[:, pl.ds(0, 512)], b0[c, z_lo, :, :, :, pl.ds(0, 768)].reshape(512, 768))
        acc = acc + mm(norm2[:, pl.ds(512, 512)], b0[c, z_lo + 2, :, :, :, pl.ds(0, 768)].reshape(512, 768))
        qkv[:, pl.ds(0, 256)] = (acc[:, :256] * 0.125).astype(BF)
        qkv[:, pl.ds(256, 512)] = acc[:, 256:].astype(BF)
        spots = [(pl.ds(144 * w, 144), 128 * h) for w in range(3) for h in range(2)]
        heads = [(qkv[r, pl.ds(c, 128)], qkv[r, pl.ds(256 + c, 128)], qkv[r, pl.ds(512 + c, 128)], None) for r, c in spots]
        for (r, c), o in zip(spots, attend_heads(heads)):
            blend[g, r, pl.ds(c, 128)] = o.astype(BF)

        @pl.when(g == 0)
        def _():
            later_events[7]()

        return carry

    lax.fori_loop(0, 4, attend_slice, 0)

    later_arrived((0, 1))
    for half in range(2):
        acc = merged[:, pl.ds(512 * half, 512)].astype(F32)
        for g in range(4):
            w_t = b1[g % 2, 2 * half + g // 2, :, :, :, pl.ds(0, 256)].reshape(512, 256)
            acc = acc + mm_nt(blend[g], w_t)
        acc = acc.astype(BF).astype(F32)
        total[2 * half] = acc[:, :256]
        total[2 * half + 1] = acc[:, 256:]
    norm2[...] = normed(jnp.concatenate([total[p] for p in range(4)], axis=1)).astype(BF)

    def widen(g, carry):
        z_lo, c = g // 2, g % 2
        u = mm(norm2[:, pl.ds(0, 512)], b1[c, z_lo, :, :, :, pl.ds(256, 1024)].reshape(512, 1024))
        u = u + mm(norm2[:, pl.ds(512, 512)], b1[c, z_lo + 2, :, :, :, pl.ds(256, 1024)].reshape(512, 1024))
        lifted[g] = gelu(u).astype(BF)
        return carry

    lax.fori_loop(0, 4, widen, 0)
    later_arrived((2,))

    mine = out.at[:, pl.ds(18 * lat, 18)]
    owners = ((lat + 2) % 4, 3 - lat, (lat // 2) * 2 + 1 - core, lat)

    def hand_out(n):
        src = result.at[owners[n]]
        if n == 3:
            return pltpu.make_async_copy(src, mine, loc.at[9])
        return remote(src, mine, fin_s.at[n], fin_r.at[n], (lon, owners[n]))

    for n in range(4):
        p = owners[n]
        acc = total[p]
        for g in range(4):
            back = b1[g % 2, g // 2 + 2 * (p // 2), pl.ds(p % 2 * 2, 2), :, :, pl.ds(1280, 1024)].reshape(256, 1024)
            acc = acc + mm_nt(lifted[g], back)
        acc = acc.astype(BF)
        for w in range(3):
            spread = mm(pad[...], acc[144 * w : 144 * w + 144]).astype(BF).reshape(12, 16, 256)
            for level in range(2):
                result[p, level, pl.ds(6 * w, 6)] = spread[6 * level : 6 * level + 6, :12]
        hand_out(n).start()

    first_drain()
    later_drain()
    for c in rim + [c for a in range(1, 6) for c in sides(a)]:
        c.wait_send()
    for n in range(4):
        hand_out(n).wait()


def choose(shape, pairs):
    out = np.zeros(shape, np.float32)
    for r, c in pairs:
        out[r, c] = 1.0
    return jnp.asarray(out, BF)


def choices():
    own, side, put, quarter = [], [], [], []
    for n, h in enumerate((0, -1, 1, 2, 3, 4)):
        for rho in range(6):
            for level in range(2):
                for c in range(6):
                    i = n * 72 + rho * 12 + level * 6 + c
                    if h < 0:
                        side.append((i, rho * 16 + level * 8 + c + 2))
                    elif h > 3:
                        side.append((i, 96 + rho * 16 + level * 8 + c))
                    else:
                        own.append((i, level * 144 + rho * 24 + h * 6 + c))
                        put.append((rho * 48 + h * 12 + level * 6 + c, h * 72 + rho * 12 + level * 6 + c))
    for pc in range(2):
        for level in range(2):
            for ii in range(6):
                for j in range(12):
                    h, c = divmod(2 * j + pc, 6)
                    quarter.append((pc * 144 + level * 72 + ii * 12 + j, ii * 48 + h * 12 + level * 6 + c))
    mix = [(blk * 64 + g * 16 + r, g * 128 + blk * 16 + r) for g in range(4) for blk in range(8) for r in range(16)]
    pad = [(g * 16 + j, g * 12 + j) for g in range(12) for j in range(12)]
    return (
        choose((432, 288), own), choose((432, 192), side), choose((288, 288), put),
        choose((288, 288), quarter), choose((512, 512), mix), choose((192, 144), pad),
    )


def window_ids(region_ids):
    lat = lax.axis_index("lat")
    lon = lax.axis_index("lon")

    def around(field, axis, place, count, size, edge):
        def cut(at, start, width):
            return lax.dynamic_slice_in_dim(field, at % count * size + start, width, axis)

        return [cut(place - 1, size - edge, edge), cut(place, 0, size), cut(place + 1, 0, edge)]

    field = jnp.concatenate(around(region_ids, 1, lat + 4, 4, 36, 3), axis=1)
    before, own, after = around(field, 2, lon + 32, 32, 24, 6)
    ids = jnp.concatenate([own[:, :, :6], before, own[:, :, 6:], after], axis=2)
    return ids.reshape(2, 7, 6, 3, 2, 6).transpose(1, 3, 4, 2, 0, 5).reshape(21, 144)


def body(
    latents, region_ids, attend_one, project_one, expand_one, reduce_one,
    merge_weight, attend_two, project_two, expand_two, reduce_two,
):
    vmem = pl.BlockSpec(memory_space=pltpu.VMEM)
    hbm = pl.BlockSpec(memory_space=pl.ANY)
    sem = pltpu.SemaphoreType.DMA
    regroup = choices()
    return pl.pallas_call(
        kernel,
        out_shape=jax.ShapeDtypeStruct((2, 72, 12, 256), BF),
        in_specs=[hbm, vmem] + [hbm] * 15,
        out_specs=hbm,
        scratch_shapes=[pltpu.VMEM((2, 4, 4, 4, 32, w), BF) for w in WIDTHS]
        + [
            pltpu.VMEM((2, 42, 24, 512), BF), pltpu.VMEM((36, 16, 512), BF), pltpu.VMEM((36, 16, 512), BF),
            pltpu.VMEM((42, 16, 512), BF), pltpu.VMEM((42, 16, 512), BF), pltpu.VMEM((42, 48, 512), BF),
            pltpu.VMEM((4, 432, 512), BF), pltpu.VMEM((432, 1024), BF), pltpu.VMEM((432, 768), BF),
            pltpu.VMEM((4, 432, 256), BF), pltpu.VMEM((432, 1024), BF),
            pltpu.VMEM((4, 432, 256), F32), pltpu.VMEM((4, 432, 1024), BF), pltpu.VMEM((4, 2, 18, 12, 256), BF),
            pltpu.VMEM((3, 512, 512), BF), pltpu.VMEM((512, 512), BF),
            pltpu.VMEM((512, 2048), BF), pltpu.VMEM((2048, 512), BF),
        ]
        + [pltpu.VMEM(m.shape, BF) for m in regroup]
        + [
            sem((6, 24)), sem((6, 24)), sem((6, 16)), sem((6, 16)), sem((12,)), sem((10,)),
            sem((20,)), sem((20,)), sem((3,)), sem((3,)),
        ],
        compiler_params=pltpu.CompilerParams(collective_id=0, has_side_effects=True, vmem_limit_bytes=63 * 2**20),
        cost_estimate=pl.CostEstimate(flops=24 * 10**9, bytes_accessed=10 * 10**6, transcendentals=10**7),
    )(
        latents, window_ids(region_ids), attend_one, project_one, expand_one, reduce_one,
        merge_weight, attend_two, project_two.T, expand_two, reduce_two.T, *regroup,
    )


def solution(mesh):
    return jax.shard_map(
        body,
        mesh=mesh,
        in_specs=(
            P(None, "lat", "lon", None), P(), P(), P(), P(), P(),
            P(("lon", "lat"), None), P(None, "lon", "lat"), P("lat", "lon"), P("lon", "lat"), P("lat", "lon"),
        ),
        out_specs=P(None, None, "lon", "lat"),
        check_vma=False,
    )
```

```python
import jax
import jax.numpy as jnp
import numpy as np
from jax import lax
from jax.experimental import pallas as pl
from jax.experimental.pallas import tpu as pltpu
from jax.sharding import PartitionSpec as P

MESH = pl.DeviceIdType.MESH
BF = jnp.bfloat16
F32 = jnp.float32
EPSILON = 1e-05
MASKED = -1e30
ORDERS = (("x", "y", "z"), ("y", "z", "x"), ("z", "x", "y"))
WIDTHS = (2560, 1024)
SPANS = (((0, 896), (896, 896), (1792, 768)), ((0, 256), (256, 384), (640, 384)))
SUB = (0, -1, 1, 2)


def gather_plan(kind, buf, send, recv, sibs, sibr):
    lon = lax.axis_index("lon")
    lat = lax.axis_index("lat")
    me = {"x": (lon // 4) % 4, "y": lon % 4, "z": (lon // 16) * 2 + lat // 2}
    core = lat % 2

    def device(pos, c):
        return ((pos["z"] // 2) * 16 + pos["x"] * 4 + pos["y"], (pos["z"] % 2) * 2 + c)

    def shifted(axis, by):
        pos = dict(me)
        pos[axis] = (me[axis] + by + 4) % 4
        return pos

    def part(s, fix, half):
        at = [slice(None) if fix[a] is None else fix[a] for a in ("z", "x", "y")]
        rows = slice(None) if half is None else pl.ds(16 * half, 16)
        return buf.at[core, at[0], at[1], at[2], rows, pl.ds(*SPANS[kind][s])]

    def copy(s, n, fix, axis, by, half=None):
        ref = part(s, fix, half)
        return pltpu.make_async_remote_copy(
            src_ref=ref, dst_ref=ref, send_sem=send.at[3 * kind + s, n], recv_sem=recv.at[3 * kind + s, n],
            device_id=device(shifted(axis, by), core), device_id_type=MESH,
        )

    def sibling(s, k, j):
        ref = part(s, group(s, 3, SUB[k], SUB[j]), None)
        return pltpu.make_async_remote_copy(
            src_ref=ref, dst_ref=ref, send_sem=sibs.at[3 * kind + s, 4 * j + k], recv_sem=sibr.at[3 * kind + s, 4 * j + k],
            device_id=device(me, 1 - core), device_id_type=MESH,
        )

    def group(s, stage, second=0, third=0):
        axes = ORDERS[s]
        fix = dict(me)
        fix[axes[0]] = None
        fix[axes[1]] = (me[axes[1]] + second + 4) % 4
        fix[axes[2]] = (me[axes[2]] + third + 4) % 4
        return fix

    def own(s, by):
        fix = dict(me)
        axis = ORDERS[s][0]
        fix[axis] = (me[axis] + by + 4) % 4
        return fix

    def first(s):
        a = ORDERS[s][0]
        return copy(s, 0, own(s, 0), a, 1), copy(s, 1, own(s, 0), a, -1)

    def first_on(s):
        a = ORDERS[s][0]
        return copy(s, 2, own(s, -1), a, 1, 0), copy(s, 3, own(s, 1), a, -1, 1)

    def second(s):
        a = ORDERS[s][1]
        return copy(s, 4, group(s, 2), a, 1), copy(s, 5, group(s, 2), a, -1)

    def second_on(s):
        a = ORDERS[s][1]
        return copy(s, 6, group(s, 2, -1), a, 1, 0), copy(s, 7, group(s, 2, 1), a, -1, 1)

    def third(s, k):
        a = ORDERS[s][2]
        fix = group(s, 3, SUB[k])
        return copy(s, 8 + 4 * k, fix, a, 1), copy(s, 9 + 4 * k, fix, a, -1)

    def third_on(s, k):
        a = ORDERS[s][2]
        return (
            copy(s, 10 + 4 * k, group(s, 3, SUB[k], -1), a, 1, 0),
            copy(s, 11 + 4 * k, group(s, 3, SUB[k], 1), a, -1, 1),
        )

    def go(copies):
        for c in copies:
            c.start()

    def got(copies):
        for c in copies:
            c.wait_recv()

    streams = range(3)

    def e0():
        for s in streams:
            go(first(s))

    def e1():
        for s in streams:
            got(first(s))
            go(first_on(s))

    def e2():
        for s in streams:
            got(first_on(s))
            go(second(s))
            go(third(s, 0))
        for s in streams:
            sibling(s, 0, 0).start()

    def e3():
        for s in streams:
            got(second(s))
            go(second_on(s))
            go(third(s, 1))
            go(third(s, 2))
        for s in streams:
            sibling(s, 1, 0).start()
            sibling(s, 2, 0).start()
        for s in streams:
            got(third(s, 0))
            go(third_on(s, 0))
            sibling(s, 0, 1).start()
            sibling(s, 0, 2).start()

    def e4():
        for s in streams:
            got(second_on(s))
            go(third(s, 3))
            sibling(s, 3, 0).start()
        for k in (1, 2):
            for s in streams:
                got(third(s, k))
                go(third_on(s, k))
                sibling(s, k, 1).start()
                sibling(s, k, 2).start()

    def e5():
        for s in streams:
            got(third_on(s, 0))
            sibling(s, 0, 3).start()
        for s in streams:
            got(third(s, 3))
            go(third_on(s, 3))
            sibling(s, 3, 1).start()
            sibling(s, 3, 2).start()

    def e6():
        for k in (1, 2):
            for s in streams:
                got(third_on(s, k))
                sibling(s, k, 3).start()

    def e7():
        for s in streams:
            got(third_on(s, 3))
            sibling(s, 3, 3).start()

    def arrived():
        for j in range(4):
            for k in range(4):
                for s in streams:
                    sibling(s, k, j).wait_recv()

    def drain():
        for s in streams:
            for c in first(s) + first_on(s) + second(s) + second_on(s):
                c.wait_send()
            for k in range(4):
                for c in third(s, k) + third_on(s, k):
                    c.wait_send()
                for j in range(4):
                    sibling(s, k, j).wait_send()

    partners = [device(shifted(a, d), core) for a in "xyz" for d in (1, -1)] + [device(me, 1 - core)]
    return me, core, (e0, e1, e2, e3, e4, e5, e6, e7), arrived, drain, partners


def normed(values):
    centered = values - jnp.mean(values, axis=-1, keepdims=True)
    variance = jnp.mean(centered * centered, axis=-1, keepdims=True)
    return centered * lax.rsqrt(variance + EPSILON)


def gelu(v):
    return 0.5 * v * (1.0 + jnp.tanh(0.7978845608028654 * (v + 0.044715 * (v * v * v))))


def mm(a, b):
    return jnp.dot(a, b, preferred_element_type=F32)


def mm_nt(a, b):
    return lax.dot_general(a, b, (((1,), (1,)), ((), ())), preferred_element_type=F32)


def attend_heads(pairs):
    is_low = lax.broadcasted_iota(jnp.int32, pairs[0][0].shape, 1) < 64
    low_f = (lax.broadcasted_iota(jnp.int32, pairs[0][1].shape, 1) < 64).astype(F32)
    low = low_f.astype(BF)
    high = (1.0 - low_f).astype(BF)
    scores = []
    for q, k, _, bias in pairs:
        for mask in (low, high):
            s = mm_nt(q, k * mask)
            scores.append(s if bias is None else s + bias)
    highest = [jnp.max(s, axis=-1, keepdims=True) for s in scores]
    lifted = [jnp.exp(s - m).astype(BF) for s, m in zip(scores, highest)]
    blends = []
    for n, (_, _, v, _) in enumerate(pairs):
        blends.append((mm(lifted[2 * n], v * low + high), mm(lifted[2 * n + 1], v * high + low)))
    outs = []
    for even, odd in blends:
        sums = pltpu.roll(jnp.where(is_low, odd, even), 64, 1)
        outs.append(jnp.where(is_low, even, odd) / sums)
    return outs


def kernel(
    latents, ids, attend_h, project_h, expand_h, shrink_h, merge_h, attend2_h, project2_h, expand2_h, reduce2_h,
    pick_own_h, pick_side_h, put_h, quarter_h, mix_h, pad_h,
    out,
    b0, b1, tile, edge_w, edge_e, cols_w, cols_e, y_rows, quart, merged, qkv, blend, norm2, total, lifted, result,
    attend, project, expand, shrink, pick_own, pick_side, put, quarter, mix, pad,
    send, recv, sibs, sibr, loc, wsem, halo_s, halo_r, fin_s, fin_r,
):
    me, core, first_events, first_arrived, first_drain, partners = gather_plan(0, b0, send, recv, sibs, sibr)
    _, _, last_events, last_arrived, last_drain, _ = gather_plan(1, b1, send, recv, sibs, sibr)
    lon = lax.axis_index("lon")
    lat = lax.axis_index("lat")
    west, east = (lon + 31) % 32, (lon + 1) % 32
    above, below = (lat + 3) % 4, (lat + 1) % 4

    fetch_tile = pltpu.make_async_copy(latents, tile.at[:, pl.ds(3, 36)], loc.at[0])
    fetch_tile.start()
    at = (core, me["z"], me["x"], me["y"])
    shards = [
        (merge_h.at[:, pl.ds(0, 512)], b0.at[at + (pl.ds(0, 16), pl.ds(768, 512))]),
        (merge_h.at[:, pl.ds(512, 512)], b0.at[at + (pl.ds(16, 16), pl.ds(768, 512))]),
    ]
    shards += [(attend2_h.at[i], b0.at[at + (slice(None), pl.ds(256 * i, 256))]) for i in range(3)]
    shards += [
        (project2_h, b0.at[at + (slice(None), pl.ds(1280, 256))]),
        (expand2_h, b0.at[at + (slice(None), pl.ds(1536, 1024))]),
        (reduce2_h, b1.at[at]),
    ]
    shards = [pltpu.make_async_copy(src, dst, loc.at[n + 1]) for n, (src, dst) in enumerate(shards)]
    for c in shards:
        c.start()
    weights = [
        pltpu.make_async_copy(src, dst, wsem.at[n])
        for n, (src, dst) in enumerate(
            (
                (pick_own_h, pick_own), (pick_side_h, pick_side), (attend_h, attend), (project_h, project), (expand_h, expand),
                (shrink_h, shrink), (put_h, put), (quarter_h, quarter), (mix_h, mix), (pad_h, pad),
            )
        )
    ]
    for c in weights:
        c.start()
    everyone = partners + [(west, lat), (east, lat), (lon, above), (lon, below), (lon, (lat + 2) % 4)]
    everyone += [(west, above), (east, below), (west, below), (east, above)]
    barrier = pltpu.get_barrier_semaphore()
    for d in everyone:
        pl.semaphore_signal(barrier, inc=1, device_id=d, device_id_type=MESH)
    fetch_tile.wait()
    for level in range(2):
        edge_w[:, pl.ds(8 * level, 8)] = tile[level, pl.ds(3, 36), pl.ds(0, 8)]
        edge_e[:, pl.ds(8 * level, 8)] = tile[level, pl.ds(3, 36), pl.ds(16, 8)]
    for c in shards:
        c.wait()
    pl.semaphore_wait(barrier, len(everyone))

    def remote(src, dst, ssem, rsem, to):
        return pltpu.make_async_remote_copy(
            src_ref=src, dst_ref=dst, send_sem=ssem, recv_sem=rsem, device_id=to, device_id_type=MESH
        )

    def halo(n, src, dst, to):
        return remote(src, dst, halo_s.at[n], halo_r.at[n], to)

    def sides(a):
        here, there = pl.ds(6 * a - 3, 6), pl.ds(6 * a, 6)
        return [
            halo(2 * a - 2, edge_w.at[here], cols_e.at[there], (west, lat)),
            halo(2 * a - 1, edge_e.at[here], cols_w.at[there], (east, lat)),
        ]

    top, low = pl.ds(0, 3), pl.ds(33, 3)
    before, after = pl.ds(0, 3), pl.ds(39, 3)
    rim = [
        halo(10, edge_w.at[top], cols_e.at[pl.ds(3, 3)], (west, lat)),
        halo(11, edge_e.at[top], cols_w.at[pl.ds(3, 3)], (east, lat)),
        halo(12, edge_w.at[low], cols_e.at[pl.ds(36, 3)], (west, lat)),
        halo(13, edge_e.at[low], cols_w.at[pl.ds(36, 3)], (east, lat)),
        halo(14, edge_w.at[top], cols_e.at[after], (west, above)),
        halo(15, edge_e.at[top], cols_w.at[after], (east, above)),
        halo(16, edge_w.at[low], cols_e.at[before], (west, below)),
        halo(17, edge_e.at[low], cols_w.at[before], (east, below)),
        halo(18, latents.at[:, top], tile.at[:, after], (lon, above)),
        halo(19, latents.at[:, low], tile.at[:, before], (lon, below)),
    ]
    first_events[0]()
    for a in (1, 2):
        for c in sides(a):
            c.start()
    last_events[0]()
    for c in sides(3):
        c.start()
    for c in weights:
        c.wait()

    f, r = first_events, last_events
    early = {
        (0, 0): (f[1],), (0, 1): (r[1],), (0, 3): (f[2],), (1, 3): (f[3],), (3, 0): (f[4],), (4, 1): (f[5],),
        (5, 0): (r[2],), (5, 1): (f[6],), (6, 1): (r[3],), (6, 3): (f[7],),
    }

    def step_events(t, half):
        for (when, which), events in early.items():
            if which == half:

                @pl.when(t == when)
                def _(events=events):
                    for event in events:
                        event()

    def strip(t, carry):
        a = jnp.where(t < 5, t + 1, (t - 5) * 6)

        @pl.when(t < 5)
        def _():
            for c in sides(t + 1):
                c.wait_recv()

        @pl.when(t == 5)
        def _():
            for c in rim:
                c.wait_recv()

        span = pl.ds(6 * a, 6)
        own = tile[:, span].astype(F32).reshape(288, 512).astype(BF)
        side = jnp.concatenate([cols_w[span].reshape(96, 512), cols_e[span].reshape(96, 512)], axis=0)
        x = mm(pick_own[...], own) + mm(pick_side[...], side)
        n = normed(x).astype(BF)
        q = (mm(n[:360], attend[0]) * 0.125).astype(BF)
        k = mm(n, attend[1]).astype(BF)
        v = mm(n, attend[2]).astype(BF)
        step_events(t, 0)
        parts = []
        for b, size in enumerate((72, 144, 72)):
            kinds = lax.broadcasted_iota(jnp.int32, (16, 144), 0)
            hot = (ids[pl.ds(3 * a + b, 1), :] == kinds).astype(F32).astype(BF)
            same = lax.dot_general(hot, hot, (((0,), (0,)), ((), ())), preferred_element_type=F32)
            bias = ((same - 1.0) * -MASKED)[:size]
            r = slice(144 * b, 144 * b + 144)
            r_q = slice(144 * b, 144 * b + size)
            heads = [(q[r_q, c : c + 128], k[r, c : c + 128], v[r, c : c + 128], bias) for c in range(0, 512, 128)]
            parts.append(jnp.concatenate(attend_heads(heads), axis=1))
        o = jnp.concatenate(parts, axis=0).astype(BF)
        x = jnp.concatenate([x[:72], x[144:360]], axis=0)
        step_events(t, 1)
        for when in range(2):

            @pl.when(t == when)
            def _(when=when):
                for c in sides(when + 4):
                    c.start()

        @pl.when(t == 2)
        def _():
            for c in rim:
                c.start()

        hid = (x + mm(o, project[...])).astype(BF)
        hid_f = hid.astype(F32)
        n = normed(hid_f).astype(BF)
        acc = hid_f
        for c in range(4):
            u = gelu(mm(n, expand[:, 512 * c : 512 * c + 512])).astype(BF)
            acc = acc + mm(u, shrink[512 * c : 512 * c + 512, :])
            if c == 1:
                step_events(t, 2)
        y_rows[span] = mm(put[...], acc.astype(BF)).astype(BF).reshape(6, 48, 512)
        step_events(t, 3)
        return carry

    lax.fori_loop(0, 7, strip, 0)

    for w in range(3):
        both = y_rows[pl.ds(12 * w + 3, 12)].reshape(6, 2, 48, 512)
        found = [mm(quarter[...], both[:, odd].reshape(288, 512)) for odd in range(2)]
        quads = [found[0][:144], found[1][:144], found[0][144:], found[1][144:]]
        mean = sum(jnp.sum(p, axis=-1, keepdims=True) for p in quads) * (1.0 / 2048.0)
        quads = [p - mean for p in quads]
        variance = sum(jnp.sum(p * p, axis=-1, keepdims=True) for p in quads) * (1.0 / 2048.0)
        scale = lax.rsqrt(variance + EPSILON)
        for p in range(4):
            quart[p, pl.ds(144 * w, 144)] = mm((quads[p] * scale).astype(BF), mix[...]).astype(BF)

    first_arrived()
    for half in range(2):
        acc = jnp.zeros((432, 512), F32)
        for z in range(4):
            for c in range(2):
                ch = slice(128 * ((z % 2) * 2 + c), 128 * ((z % 2) * 2 + c) + 128)
                left = jnp.concatenate([quart[z // 2 * 2, :, ch], quart[z // 2 * 2 + 1, :, ch]], axis=1)
                right = b0[c, z, :, :, pl.ds(16 * half, 16), pl.ds(768, 512)].reshape(256, 512)
                acc = acc + mm(left, right)
        merged[:, pl.ds(512 * half, 512)] = acc.astype(BF)

    last_events[4]()
    norm2[...] = normed(merged[...].astype(F32)).astype(BF)

    def attend_slice(g, carry):
        z_lo, c = g // 2, g % 2
        acc = mm(norm2[:, pl.ds(0, 512)], b0[c, z_lo, :, :, :, pl.ds(0, 768)].reshape(512, 768))
        acc = acc + mm(norm2[:, pl.ds(512, 512)], b0[c, z_lo + 2, :, :, :, pl.ds(0, 768)].reshape(512, 768))
        qkv[:, pl.ds(0, 256)] = (acc[:, :256] * 0.125).astype(BF)
        qkv[:, pl.ds(256, 512)] = acc[:, 256:].astype(BF)
        spots = [(pl.ds(144 * w, 144), 128 * h) for w in range(3) for h in range(2)]
        heads = [(qkv[r, pl.ds(c, 128)], qkv[r, pl.ds(256 + c, 128)], qkv[r, pl.ds(512 + c, 128)], None) for r, c in spots]
        for (r, c), o in zip(spots, attend_heads(heads)):
            blend[g, r, pl.ds(c, 128)] = o.astype(BF)

        @pl.when(g == 1)
        def _():
            last_events[5]()

        @pl.when(g == 3)
        def _():
            last_events[6]()

        return carry

    lax.fori_loop(0, 4, attend_slice, 0)

    for half in range(2):
        acc = merged[:, pl.ds(512 * half, 512)].astype(F32)
        for g in range(4):
            w_t = b0[g % 2, 2 * half + g // 2, :, :, :, pl.ds(1280, 256)].reshape(512, 256)
            acc = acc + mm_nt(blend[g], w_t)
        acc = acc.astype(BF).astype(F32)
        total[2 * half] = acc[:, :256]
        total[2 * half + 1] = acc[:, 256:]
    norm2[...] = normed(jnp.concatenate([total[p] for p in range(4)], axis=1)).astype(BF)

    def widen(g, carry):
        z_lo, c = g // 2, g % 2
        u = mm(norm2[:, pl.ds(0, 512)], b0[c, z_lo, :, :, :, pl.ds(1536, 1024)].reshape(512, 1024))
        u = u + mm(norm2[:, pl.ds(512, 512)], b0[c, z_lo + 2, :, :, :, pl.ds(1536, 1024)].reshape(512, 1024))
        lifted[g] = gelu(u).astype(BF)
        return carry

    lax.fori_loop(0, 4, widen, 0)
    last_events[7]()
    last_arrived()

    mine = out.at[:, pl.ds(18 * lat, 18)]
    owners = ((lat + 2) % 4, 3 - lat, (lat // 2) * 2 + 1 - core, lat)

    def hand_out(n):
        src = result.at[owners[n]]
        if n == 3:
            return pltpu.make_async_copy(src, mine, loc.at[9])
        return remote(src, mine, fin_s.at[n], fin_r.at[n], (lon, owners[n]))

    for n in range(4):
        p = owners[n]
        acc = total[p]
        for g in range(4):
            back = b1[g % 2, g // 2 + 2 * (p // 2), pl.ds(p % 2 * 2, 2)].reshape(256, 1024)
            acc = acc + mm_nt(lifted[g], back)
        acc = acc.astype(BF)
        for w in range(3):
            spread = mm(pad[...], acc[144 * w : 144 * w + 144]).astype(BF).reshape(12, 16, 256)
            for level in range(2):
                result[p, level, pl.ds(6 * w, 6)] = spread[6 * level : 6 * level + 6, :12]
        hand_out(n).start()

    first_drain()
    last_drain()
    for c in rim + [c for a in range(1, 6) for c in sides(a)]:
        c.wait_send()
    for n in range(4):
        hand_out(n).wait()


def choose(shape, pairs):
    out = np.zeros(shape, np.float32)
    for r, c in pairs:
        out[r, c] = 1.0
    return jnp.asarray(out, BF)


def choices():
    own, side, put, quarter = [], [], [], []
    for n, h in enumerate((0, -1, 1, 2, 3, 4)):
        for rho in range(6):
            for level in range(2):
                for c in range(6):
                    i = n * 72 + rho * 12 + level * 6 + c
                    if h < 0:
                        side.append((i, rho * 16 + level * 8 + c + 2))
                    elif h > 3:
                        side.append((i, 96 + rho * 16 + level * 8 + c))
                    else:
                        own.append((i, level * 144 + rho * 24 + h * 6 + c))
                        put.append((rho * 48 + h * 12 + level * 6 + c, h * 72 + rho * 12 + level * 6 + c))
    for pc in range(2):
        for level in range(2):
            for ii in range(6):
                for j in range(12):
                    h, c = divmod(2 * j + pc, 6)
                    quarter.append((pc * 144 + level * 72 + ii * 12 + j, ii * 48 + h * 12 + level * 6 + c))
    mix = [(blk * 64 + g * 16 + r, g * 128 + blk * 16 + r) for g in range(4) for blk in range(8) for r in range(16)]
    pad = [(g * 16 + j, g * 12 + j) for g in range(12) for j in range(12)]
    return (
        choose((432, 288), own), choose((432, 192), side), choose((288, 288), put),
        choose((288, 288), quarter), choose((512, 512), mix), choose((192, 144), pad),
    )


def window_ids(region_ids):
    lat = lax.axis_index("lat")
    lon = lax.axis_index("lon")

    def around(field, axis, place, count, size, edge):
        def cut(at, start, width):
            return lax.dynamic_slice_in_dim(field, at % count * size + start, width, axis)

        return [cut(place - 1, size - edge, edge), cut(place, 0, size), cut(place + 1, 0, edge)]

    field = jnp.concatenate(around(region_ids, 1, lat + 4, 4, 36, 3), axis=1)
    before, own, after = around(field, 2, lon + 32, 32, 24, 6)
    ids = jnp.concatenate([own[:, :, :6], before, own[:, :, 6:], after], axis=2)
    return ids.reshape(2, 7, 6, 3, 2, 6).transpose(1, 3, 4, 2, 0, 5).reshape(21, 144)


def body(
    latents, region_ids, attend_one, project_one, expand_one, reduce_one,
    merge_weight, attend_two, project_two, expand_two, reduce_two,
):
    vmem = pl.BlockSpec(memory_space=pltpu.VMEM)
    hbm = pl.BlockSpec(memory_space=pl.ANY)
    sem = pltpu.SemaphoreType.DMA
    regroup = choices()
    return pl.pallas_call(
        kernel,
        out_shape=jax.ShapeDtypeStruct((2, 72, 12, 256), BF),
        in_specs=[hbm, vmem] + [hbm] * 15,
        out_specs=hbm,
        scratch_shapes=[pltpu.VMEM((2, 4, 4, 4, 32, w), BF) for w in WIDTHS]
        + [
            pltpu.VMEM((2, 42, 24, 512), BF), pltpu.VMEM((36, 16, 512), BF), pltpu.VMEM((36, 16, 512), BF),
            pltpu.VMEM((42, 16, 512), BF), pltpu.VMEM((42, 16, 512), BF), pltpu.VMEM((42, 48, 512), BF),
            pltpu.VMEM((4, 432, 512), BF), pltpu.VMEM((432, 1024), BF), pltpu.VMEM((432, 768), BF),
            pltpu.VMEM((4, 432, 256), BF), pltpu.VMEM((432, 1024), BF),
            pltpu.VMEM((4, 432, 256), F32), pltpu.VMEM((4, 432, 1024), BF), pltpu.VMEM((4, 2, 18, 12, 256), BF),
            pltpu.VMEM((3, 512, 512), BF), pltpu.VMEM((512, 512), BF),
            pltpu.VMEM((512, 2048), BF), pltpu.VMEM((2048, 512), BF),
        ]
        + [pltpu.VMEM(m.shape, BF) for m in regroup]
        + [
            sem((6, 24)), sem((6, 24)), sem((6, 16)), sem((6, 16)), sem((12,)), sem((10,)),
            sem((20,)), sem((20,)), sem((3,)), sem((3,)),
        ],
        compiler_params=pltpu.CompilerParams(collective_id=0, has_side_effects=True, vmem_limit_bytes=63 * 2**20),
        cost_estimate=pl.CostEstimate(flops=24 * 10**9, bytes_accessed=10 * 10**6, transcendentals=10**7),
    )(
        latents, window_ids(region_ids), attend_one, project_one, expand_one, reduce_one,
        merge_weight, attend_two, project_two.T, expand_two, reduce_two.T, *regroup,
    )


def solution(mesh):
    return jax.shard_map(
        body,
        mesh=mesh,
        in_specs=(
            P(None, "lat", "lon", None), P(), P(), P(), P(), P(),
            P(("lon", "lat"), None), P(None, "lon", "lat"), P("lat", "lon"), P("lon", "lat"), P("lat", "lon"),
        ),
        out_specs=P(None, None, "lon", "lat"),
        check_vma=False,
    )
```

```python
import jax
import jax.numpy as jnp
import numpy as np
from jax import lax
from jax.experimental import pallas as pl
from jax.experimental.pallas import tpu as pltpu
from jax.sharding import PartitionSpec as P

MESH = pl.DeviceIdType.MESH
BF = jnp.bfloat16
F32 = jnp.float32
EPSILON = 1e-05
MASKED = -1e30
ORDERS = (("x", "y", "z"), ("y", "z", "x"), ("z", "x", "y"))
WIDTHS = (2560, 1024)
SPANS = (((0, 896), (896, 896), (1792, 768)), ((0, 256), (256, 384), (640, 384)))
SUB = (0, -1, 1, 2)


def gather_plan(kind, buf, send, recv, sibs, sibr):
    lon = lax.axis_index("lon")
    lat = lax.axis_index("lat")
    me = {"x": (lon // 4) % 4, "y": lon % 4, "z": (lon // 16) * 2 + lat // 2}
    core = lat % 2

    def device(pos, c):
        return ((pos["z"] // 2) * 16 + pos["x"] * 4 + pos["y"], (pos["z"] % 2) * 2 + c)

    def shifted(axis, by):
        pos = dict(me)
        pos[axis] = (me[axis] + by + 4) % 4
        return pos

    def part(s, fix, half):
        at = [slice(None) if fix[a] is None else fix[a] for a in ("z", "x", "y")]
        rows = slice(None) if half is None else pl.ds(16 * half, 16)
        return buf.at[core, at[0], at[1], at[2], rows, pl.ds(*SPANS[kind][s])]

    def copy(s, n, fix, axis, by, half=None):
        ref = part(s, fix, half)
        return pltpu.make_async_remote_copy(
            src_ref=ref, dst_ref=ref, send_sem=send.at[3 * kind + s, n], recv_sem=recv.at[3 * kind + s, n],
            device_id=device(shifted(axis, by), core), device_id_type=MESH,
        )

    def sibling(s, k, j):
        ref = part(s, group(s, 3, SUB[k], SUB[j]), None)
        return pltpu.make_async_remote_copy(
            src_ref=ref, dst_ref=ref, send_sem=sibs.at[3 * kind + s, 4 * j + k], recv_sem=sibr.at[3 * kind + s, 4 * j + k],
            device_id=device(me, 1 - core), device_id_type=MESH,
        )

    def group(s, stage, second=0, third=0):
        axes = ORDERS[s]
        fix = dict(me)
        fix[axes[0]] = None
        fix[axes[1]] = (me[axes[1]] + second + 4) % 4
        fix[axes[2]] = (me[axes[2]] + third + 4) % 4
        return fix

    def own(s, by):
        fix = dict(me)
        axis = ORDERS[s][0]
        fix[axis] = (me[axis] + by + 4) % 4
        return fix

    def first(s):
        a = ORDERS[s][0]
        return copy(s, 0, own(s, 0), a, 1), copy(s, 1, own(s, 0), a, -1)

    def first_on(s):
        a = ORDERS[s][0]
        return copy(s, 2, own(s, -1), a, 1, 0), copy(s, 3, own(s, 1), a, -1, 1)

    def second(s):
        a = ORDERS[s][1]
        return copy(s, 4, group(s, 2), a, 1), copy(s, 5, group(s, 2), a, -1)

    def second_on(s):
        a = ORDERS[s][1]
        return copy(s, 6, group(s, 2, -1), a, 1, 0), copy(s, 7, group(s, 2, 1), a, -1, 1)

    def third(s, k):
        a = ORDERS[s][2]
        fix = group(s, 3, SUB[k])
        return copy(s, 8 + 4 * k, fix, a, 1), copy(s, 9 + 4 * k, fix, a, -1)

    def third_on(s, k):
        a = ORDERS[s][2]
        return (
            copy(s, 10 + 4 * k, group(s, 3, SUB[k], -1), a, 1, 0),
            copy(s, 11 + 4 * k, group(s, 3, SUB[k], 1), a, -1, 1),
        )

    def go(copies):
        for c in copies:
            c.start()

    def got(copies):
        for c in copies:
            c.wait_recv()

    streams = range(3)

    def e0():
        for s in streams:
            go(first(s))

    def e1():
        for s in streams:
            got(first(s))
            go(first_on(s))

    def e2():
        for s in streams:
            got(first_on(s))
            go(second(s))
            go(third(s, 0))
        for s in streams:
            sibling(s, 0, 0).start()

    def e3():
        for s in streams:
            got(second(s))
            go(second_on(s))
            go(third(s, 1))
            go(third(s, 2))
        for s in streams:
            sibling(s, 1, 0).start()
            sibling(s, 2, 0).start()
        for s in streams:
            got(third(s, 0))
            go(third_on(s, 0))
            sibling(s, 0, 1).start()
            sibling(s, 0, 2).start()

    def e4():
        for s in streams:
            got(second_on(s))
            go(third(s, 3))
            sibling(s, 3, 0).start()
        for k in (1, 2):
            for s in streams:
                got(third(s, k))
                go(third_on(s, k))
                sibling(s, k, 1).start()
                sibling(s, k, 2).start()

    def e5():
        for s in streams:
            got(third_on(s, 0))
            sibling(s, 0, 3).start()
        for s in streams:
            got(third(s, 3))
            go(third_on(s, 3))
            sibling(s, 3, 1).start()
            sibling(s, 3, 2).start()

    def e6():
        for k in (1, 2):
            for s in streams:
                got(third_on(s, k))
                sibling(s, k, 3).start()

    def e7():
        for s in streams:
            got(third_on(s, 3))
            sibling(s, 3, 3).start()

    def arrived():
        for j in range(4):
            for k in range(4):
                for s in streams:
                    sibling(s, k, j).wait_recv()

    def drain():
        for s in streams:
            for c in first(s) + first_on(s) + second(s) + second_on(s):
                c.wait_send()
            for k in range(4):
                for c in third(s, k) + third_on(s, k):
                    c.wait_send()
                for j in range(4):
                    sibling(s, k, j).wait_send()

    partners = [device(shifted(a, d), core) for a in "xyz" for d in (1, -1)] + [device(me, 1 - core)]
    return me, core, (e0, e1, e2, e3, e4, e5, e6, e7), arrived, drain, partners


def normed(values):
    centered = values - jnp.mean(values, axis=-1, keepdims=True)
    variance = jnp.mean(centered * centered, axis=-1, keepdims=True)
    return centered * lax.rsqrt(variance + EPSILON)


def gelu(v):
    return 0.5 * v * (1.0 + jnp.tanh(0.7978845608028654 * (v + 0.044715 * (v * v * v))))


def mm(a, b):
    return jnp.dot(a, b, preferred_element_type=F32)


def mm_nt(a, b):
    return lax.dot_general(a, b, (((1,), (1,)), ((), ())), preferred_element_type=F32)


def attend_heads(pairs):
    is_low = lax.broadcasted_iota(jnp.int32, pairs[0][0].shape, 1) < 64
    low_f = (lax.broadcasted_iota(jnp.int32, pairs[0][1].shape, 1) < 64).astype(F32)
    low = low_f.astype(BF)
    high = (1.0 - low_f).astype(BF)
    scores = []
    for q, k, _, bias in pairs:
        for mask in (low, high):
            s = mm_nt(q, k * mask)
            scores.append(s if bias is None else s + bias)
    highest = [jnp.max(s, axis=-1, keepdims=True) for s in scores]
    lifted = [jnp.exp(s - m).astype(BF) for s, m in zip(scores, highest)]
    blends = []
    for n, (_, _, v, _) in enumerate(pairs):
        blends.append((mm(lifted[2 * n], v * low + high), mm(lifted[2 * n + 1], v * high + low)))
    outs = []
    for even, odd in blends:
        sums = pltpu.roll(jnp.where(is_low, odd, even), 64, 1)
        outs.append(jnp.where(is_low, even, odd) / sums)
    return outs


def kernel(
    latents, ids, attend_h, project_h, expand_h, shrink_h, merge_h, attend2_h, project2_h, expand2_h, reduce2_h,
    pick_own_h, pick_side_h, put_h, quarter_h, mix_h, pad_h,
    out,
    b0, b1, tile, edge_w, edge_e, cols_w, cols_e, y_rows, quart, merged, qkv, blend, norm2, total, lifted, result,
    attend, project, expand, shrink, pick_own, pick_side, put, quarter, mix, pad,
    send, recv, sibs, sibr, loc, wsem, halo_s, halo_r, fin_s, fin_r,
):
    me, core, first_events, first_arrived, first_drain, partners = gather_plan(0, b0, send, recv, sibs, sibr)
    _, _, last_events, last_arrived, last_drain, _ = gather_plan(1, b1, send, recv, sibs, sibr)
    lon = lax.axis_index("lon")
    lat = lax.axis_index("lat")
    west, east = (lon + 31) % 32, (lon + 1) % 32
    above, below = (lat + 3) % 4, (lat + 1) % 4

    fetch_tile = pltpu.make_async_copy(latents, tile.at[:, pl.ds(3, 36)], loc.at[0])
    fetch_tile.start()
    at = (core, me["z"], me["x"], me["y"])
    shards = [
        (merge_h.at[:, pl.ds(0, 512)], b0.at[at + (pl.ds(0, 16), pl.ds(768, 512))]),
        (merge_h.at[:, pl.ds(512, 512)], b0.at[at + (pl.ds(16, 16), pl.ds(768, 512))]),
    ]
    shards += [(attend2_h.at[i], b0.at[at + (slice(None), pl.ds(256 * i, 256))]) for i in range(3)]
    shards += [
        (project2_h, b0.at[at + (slice(None), pl.ds(1280, 256))]),
        (expand2_h, b0.at[at + (slice(None), pl.ds(1536, 1024))]),
        (reduce2_h, b1.at[at]),
    ]
    shards = [pltpu.make_async_copy(src, dst, loc.at[n + 1]) for n, (src, dst) in enumerate(shards)]
    for c in shards:
        c.start()
    weights = [
        pltpu.make_async_copy(src, dst, wsem.at[n])
        for n, (src, dst) in enumerate(
            (
                (pick_own_h, pick_own), (pick_side_h, pick_side), (attend_h, attend), (project_h, project), (expand_h, expand),
                (shrink_h, shrink), (put_h, put), (quarter_h, quarter), (mix_h, mix), (pad_h, pad),
            )
        )
    ]
    for c in weights:
        c.start()
    everyone = partners + [(west, lat), (east, lat), (lon, above), (lon, below), (lon, (lat + 2) % 4)]
    everyone += [(west, above), (east, below), (west, below), (east, above)]
    barrier = pltpu.get_barrier_semaphore()
    for d in everyone:
        pl.semaphore_signal(barrier, inc=1, device_id=d, device_id_type=MESH)
    fetch_tile.wait()
    for level in range(2):
        edge_w[:, pl.ds(8 * level, 8)] = tile[level, pl.ds(3, 36), pl.ds(0, 8)]
        edge_e[:, pl.ds(8 * level, 8)] = tile[level, pl.ds(3, 36), pl.ds(16, 8)]
    for c in shards:
        c.wait()
    pl.semaphore_wait(barrier, len(everyone))

    def remote(src, dst, ssem, rsem, to):
        return pltpu.make_async_remote_copy(
            src_ref=src, dst_ref=dst, send_sem=ssem, recv_sem=rsem, device_id=to, device_id_type=MESH
        )

    def halo(n, src, dst, to):
        return remote(src, dst, halo_s.at[n], halo_r.at[n], to)

    def sides(a):
        here, there = pl.ds(6 * a - 3, 6), pl.ds(6 * a, 6)
        return [
            halo(2 * a - 2, edge_w.at[here], cols_e.at[there], (west, lat)),
            halo(2 * a - 1, edge_e.at[here], cols_w.at[there], (east, lat)),
        ]

    top, low = pl.ds(0, 3), pl.ds(33, 3)
    before, after = pl.ds(0, 3), pl.ds(39, 3)
    rim = [
        halo(10, edge_w.at[top], cols_e.at[pl.ds(3, 3)], (west, lat)),
        halo(11, edge_e.at[top], cols_w.at[pl.ds(3, 3)], (east, lat)),
        halo(12, edge_w.at[low], cols_e.at[pl.ds(36, 3)], (west, lat)),
        halo(13, edge_e.at[low], cols_w.at[pl.ds(36, 3)], (east, lat)),
        halo(14, edge_w.at[top], cols_e.at[after], (west, above)),
        halo(15, edge_e.at[top], cols_w.at[after], (east, above)),
        halo(16, edge_w.at[low], cols_e.at[before], (west, below)),
        halo(17, edge_e.at[low], cols_w.at[before], (east, below)),
        halo(18, latents.at[:, top], tile.at[:, after], (lon, above)),
        halo(19, latents.at[:, low], tile.at[:, before], (lon, below)),
    ]
    first_events[0]()
    for a in (1, 2):
        for c in sides(a):
            c.start()
    last_events[0]()
    for c in sides(3):
        c.start()
    for c in weights:
        c.wait()

    f, r = first_events, last_events
    early = {
        (0, 0): (f[1],), (0, 1): (r[1],), (0, 3): (f[2],), (1, 3): (f[3],), (3, 0): (f[4],), (4, 1): (f[5],),
        (5, 0): (r[2],), (5, 1): (f[6],), (6, 1): (r[3],), (6, 3): (f[7],),
    }

    def step_events(t, half):
        for (when, which), events in early.items():
            if which == half:

                @pl.when(t == when)
                def _(events=events):
                    for event in events:
                        event()

    def strip(t, carry):
        a = jnp.where(t < 5, t + 1, (t - 5) * 6)

        @pl.when(t < 5)
        def _():
            for c in sides(t + 1):
                c.wait_recv()

        @pl.when(t == 5)
        def _():
            for c in rim:
                c.wait_recv()

        span = pl.ds(6 * a, 6)
        own = tile[:, span].astype(F32).reshape(288, 512).astype(BF)
        side = jnp.concatenate([cols_w[span].reshape(96, 512), cols_e[span].reshape(96, 512)], axis=0)
        x = mm(pick_own[...], own) + mm(pick_side[...], side)
        n = normed(x).astype(BF)
        q = (mm(n[:360], attend[0]) * 0.125).astype(BF)
        k = mm(n, attend[1]).astype(BF)
        v = mm(n, attend[2]).astype(BF)
        step_events(t, 0)
        parts = []
        for b, size in enumerate((72, 144, 72)):
            kinds = lax.broadcasted_iota(jnp.int32, (16, 144), 0)
            hot = (ids[pl.ds(3 * a + b, 1), :] == kinds).astype(F32).astype(BF)
            same = lax.dot_general(hot, hot, (((0,), (0,)), ((), ())), preferred_element_type=F32)
            bias = ((same - 1.0) * -MASKED)[:size]
            r = slice(144 * b, 144 * b + 144)
            r_q = slice(144 * b, 144 * b + size)
            heads = [(q[r_q, c : c + 128], k[r, c : c + 128], v[r, c : c + 128], bias) for c in range(0, 512, 128)]
            parts.append(jnp.concatenate(attend_heads(heads), axis=1))
        o = jnp.concatenate(parts, axis=0).astype(BF)
        x = jnp.concatenate([x[:72], x[144:360]], axis=0)
        step_events(t, 1)
        for when in range(2):

            @pl.when(t == when)
            def _(when=when):
                for c in sides(when + 4):
                    c.start()

        @pl.when(t == 2)
        def _():
            for c in rim:
                c.start()

        hid = (x + mm(o, project[...])).astype(BF)
        hid_f = hid.astype(F32)
        n = normed(hid_f).astype(BF)
        acc = hid_f
        for c in range(4):
            u = gelu(mm(n, expand[:, 512 * c : 512 * c + 512])).astype(BF)
            acc = acc + mm(u, shrink[512 * c : 512 * c + 512, :])
            if c == 1:
                step_events(t, 2)
        y_rows[span] = mm(put[...], acc.astype(BF)).astype(BF).reshape(6, 48, 512)
        step_events(t, 3)
        return carry

    lax.fori_loop(0, 7, strip, 0)

    for w in range(3):
        both = y_rows[pl.ds(12 * w + 3, 12)].reshape(6, 2, 48, 512)
        found = [mm(quarter[...], both[:, odd].reshape(288, 512)) for odd in range(2)]
        quads = [found[0][:144], found[1][:144], found[0][144:], found[1][144:]]
        mean = sum(jnp.sum(p, axis=-1, keepdims=True) for p in quads) * (1.0 / 2048.0)
        quads = [p - mean for p in quads]
        variance = sum(jnp.sum(p * p, axis=-1, keepdims=True) for p in quads) * (1.0 / 2048.0)
        scale = lax.rsqrt(variance + EPSILON)
        for p in range(4):
            quart[p, pl.ds(144 * w, 144)] = mm((quads[p] * scale).astype(BF), mix[...]).astype(BF)

    first_arrived()
    for half in range(2):
        acc = jnp.zeros((432, 512), F32)
        for z in range(4):
            for c in range(2):
                ch = slice(128 * ((z % 2) * 2 + c), 128 * ((z % 2) * 2 + c) + 128)
                left = jnp.concatenate([quart[z // 2 * 2, :, ch], quart[z // 2 * 2 + 1, :, ch]], axis=1)
                right = b0[c, z, :, :, pl.ds(16 * half, 16), pl.ds(768, 512)].reshape(256, 512)
                acc = acc + mm(left, right)
        merged[:, pl.ds(512 * half, 512)] = acc.astype(BF)

    last_events[4]()
    norm2[...] = normed(merged[...].astype(F32)).astype(BF)

    def attend_slice(g, carry):
        z_lo, c = g // 2, g % 2
        acc = mm(norm2[:, pl.ds(0, 512)], b0[c, z_lo, :, :, :, pl.ds(0, 768)].reshape(512, 768))
        acc = acc + mm(norm2[:, pl.ds(512, 512)], b0[c, z_lo + 2, :, :, :, pl.ds(0, 768)].reshape(512, 768))
        qkv[:, pl.ds(0, 256)] = (acc[:, :256] * 0.125).astype(BF)
        qkv[:, pl.ds(256, 512)] = acc[:, 256:].astype(BF)
        spots = [(pl.ds(144 * w, 144), 128 * h) for w in range(3) for h in range(2)]
        heads = [(qkv[r, pl.ds(c, 128)], qkv[r, pl.ds(256 + c, 128)], qkv[r, pl.ds(512 + c, 128)], None) for r, c in spots]
        for (r, c), o in zip(spots, attend_heads(heads)):
            blend[g, r, pl.ds(c, 128)] = o.astype(BF)

        @pl.when(g == 1)
        def _():
            last_events[5]()

        @pl.when(g == 3)
        def _():
            last_events[6]()

        return carry

    lax.fori_loop(0, 4, attend_slice, 0)

    for half in range(2):
        acc = merged[:, pl.ds(512 * half, 512)].astype(F32)
        for g in range(4):
            w_t = b0[g % 2, 2 * half + g // 2, :, :, :, pl.ds(1280, 256)].reshape(512, 256)
            acc = acc + mm_nt(blend[g], w_t)
        acc = acc.astype(BF).astype(F32)
        total[2 * half] = acc[:, :256]
        total[2 * half + 1] = acc[:, 256:]
    norm2[...] = normed(jnp.concatenate([total[p] for p in range(4)], axis=1)).astype(BF)

    def widen(g, carry):
        z_lo, c = g // 2, g % 2
        u = mm(norm2[:, pl.ds(0, 512)], b0[c, z_lo, :, :, :, pl.ds(1536, 1024)].reshape(512, 1024))
        u = u + mm(norm2[:, pl.ds(512, 512)], b0[c, z_lo + 2, :, :, :, pl.ds(1536, 1024)].reshape(512, 1024))
        lifted[g] = gelu(u).astype(BF)
        return carry

    lax.fori_loop(0, 4, widen, 0)
    last_events[7]()
    last_arrived()

    mine = out.at[:, pl.ds(18 * lat, 18)]
    owners = ((lat + 2) % 4, 3 - lat, (lat // 2) * 2 + 1 - core, lat)

    def hand_out(n):
        src = result.at[owners[n]]
        if n == 3:
            return pltpu.make_async_copy(src, mine, loc.at[9])
        return remote(src, mine, fin_s.at[n], fin_r.at[n], (lon, owners[n]))

    for n in range(4):
        p = owners[n]
        acc = total[p]
        for g in range(4):
            back = b1[g % 2, g // 2 + 2 * (p // 2), pl.ds(p % 2 * 2, 2)].reshape(256, 1024)
            acc = acc + mm_nt(lifted[g], back)
        acc = acc.astype(BF)
        for w in range(3):
            spread = mm(pad[...], acc[144 * w : 144 * w + 144]).astype(BF).reshape(12, 16, 256)
            for level in range(2):
                result[p, level, pl.ds(6 * w, 6)] = spread[6 * level : 6 * level + 6, :12]
        hand_out(n).start()

    first_drain()
    last_drain()
    for c in rim + [c for a in range(1, 6) for c in sides(a)]:
        c.wait_send()
    for n in range(4):
        hand_out(n).wait()


def choose(shape, pairs):
    out = np.zeros(shape, np.float32)
    for r, c in pairs:
        out[r, c] = 1.0
    return jnp.asarray(out, BF)


def choices():
    own, side, put, quarter = [], [], [], []
    for n, h in enumerate((0, -1, 1, 2, 3, 4)):
        for rho in range(6):
            for level in range(2):
                for c in range(6):
                    i = n * 72 + rho * 12 + level * 6 + c
                    if h < 0:
                        side.append((i, rho * 16 + level * 8 + c + 2))
                    elif h > 3:
                        side.append((i, 96 + rho * 16 + level * 8 + c))
                    else:
                        own.append((i, level * 144 + rho * 24 + h * 6 + c))
                        put.append((rho * 48 + h * 12 + level * 6 + c, h * 72 + rho * 12 + level * 6 + c))
    for pc in range(2):
        for level in range(2):
            for ii in range(6):
                for j in range(12):
                    h, c = divmod(2 * j + pc, 6)
                    quarter.append((pc * 144 + level * 72 + ii * 12 + j, ii * 48 + h * 12 + level * 6 + c))
    mix = [(blk * 64 + g * 16 + r, g * 128 + blk * 16 + r) for g in range(4) for blk in range(8) for r in range(16)]
    pad = [(g * 16 + j, g * 12 + j) for g in range(12) for j in range(12)]
    return (
        choose((432, 288), own), choose((432, 192), side), choose((288, 288), put),
        choose((288, 288), quarter), choose((512, 512), mix), choose((192, 144), pad),
    )


def window_ids(region_ids):
    lat = lax.axis_index("lat")
    lon = lax.axis_index("lon")

    def around(field, axis, place, count, size, edge):
        def cut(at, start, width):
            return lax.dynamic_slice_in_dim(field, at % count * size + start, width, axis)

        return [cut(place - 1, size - edge, edge), cut(place, 0, size), cut(place + 1, 0, edge)]

    field = jnp.concatenate(around(region_ids, 1, lat + 4, 4, 36, 3), axis=1)
    before, own, after = around(field, 2, lon + 32, 32, 24, 6)
    ids = jnp.concatenate([own[:, :, :6], before, own[:, :, 6:], after], axis=2)
    return ids.reshape(2, 7, 6, 3, 2, 6).transpose(1, 3, 4, 2, 0, 5).reshape(21, 144)


def body(
    latents, region_ids, attend_one, project_one, expand_one, reduce_one,
    merge_weight, attend_two, project_two, expand_two, reduce_two,
):
    vmem = pl.BlockSpec(memory_space=pltpu.VMEM)
    hbm = pl.BlockSpec(memory_space=pl.ANY)
    sem = pltpu.SemaphoreType.DMA
    regroup = choices()
    return pl.pallas_call(
        kernel,
        out_shape=jax.ShapeDtypeStruct((2, 72, 12, 256), BF),
        in_specs=[hbm, vmem] + [hbm] * 15,
        out_specs=vmem,
        scratch_shapes=[pltpu.VMEM((2, 4, 4, 4, 32, w), BF) for w in WIDTHS]
        + [
            pltpu.VMEM((2, 42, 24, 512), BF), pltpu.VMEM((36, 16, 512), BF), pltpu.VMEM((36, 16, 512), BF),
            pltpu.VMEM((42, 16, 512), BF), pltpu.VMEM((42, 16, 512), BF), pltpu.VMEM((42, 48, 512), BF),
            pltpu.VMEM((4, 432, 512), BF), pltpu.VMEM((432, 1024), BF), pltpu.VMEM((432, 768), BF),
            pltpu.VMEM((4, 432, 256), BF), pltpu.VMEM((432, 1024), BF),
            pltpu.VMEM((4, 432, 256), F32), pltpu.VMEM((4, 432, 1024), BF), pltpu.VMEM((4, 2, 18, 12, 256), BF),
            pltpu.VMEM((3, 512, 512), BF), pltpu.VMEM((512, 512), BF),
            pltpu.VMEM((512, 2048), BF), pltpu.VMEM((2048, 512), BF),
        ]
        + [pltpu.VMEM(m.shape, BF) for m in regroup]
        + [
            sem((6, 24)), sem((6, 24)), sem((6, 16)), sem((6, 16)), sem((12,)), sem((10,)),
            sem((20,)), sem((20,)), sem((3,)), sem((3,)),
        ],
        compiler_params=pltpu.CompilerParams(collective_id=0, has_side_effects=True, vmem_limit_bytes=63 * 2**20),
        cost_estimate=pl.CostEstimate(flops=24 * 10**9, bytes_accessed=10 * 10**6, transcendentals=10**7),
    )(
        latents, window_ids(region_ids), attend_one, project_one, expand_one, reduce_one,
        merge_weight, attend_two, project_two.T, expand_two, reduce_two.T, *regroup,
    )


def solution(mesh):
    return jax.shard_map(
        body,
        mesh=mesh,
        in_specs=(
            P(None, "lat", "lon", None), P(), P(), P(), P(), P(),
            P(("lon", "lat"), None), P(None, "lon", "lat"), P("lat", "lon"), P("lon", "lat"), P("lat", "lon"),
        ),
        out_specs=P(None, None, "lon", "lat"),
        check_vma=False,
    )
```
